32 devices in a mesh: ctx: 16 (over z, x, core), tp: 2 (over y).
Axes of the slice: x: 2, y: 2, z: 4, core: 2. Of those that a mesh axis runs over, the one named last changes fastest.
Arguments:
- query: bfloat16 [2048, 4096], P(('ctx', 'tp')), may hold values from -200 to 200
- keys: bfloat16 [2048, 1024], P(('ctx', 'tp')), may hold values from -20 to 20
- values: bfloat16 [2048, 1024], P(('ctx', 'tp')), may hold values from -6 to 6
- output_gradient: bfloat16 [2048, 4096], P(('ctx', 'tp')), may hold values from -6 to 6
Outputs:
- attn_out: bfloat16 [2048, 4096], P(('ctx', 'tp'))
- grad_query: bfloat16 [2048, 4096], P(('ctx', 'tp'))
- key_gradient: bfloat16 [2048, 1024], P(('ctx', 'tp'))
- value_gradient: bfloat16 [2048, 1024], P(('ctx', 'tp'))
The draws below stay inside these ranges and needn't reach their ends.
All inputs are finite; a program needn't handle non-finite values.
Results may differ from the reference program's by a relative error of at most 0.025.
Values may be sent and summed in bfloat16 or wider, within the bound.
A program may use at most 64 MiB of HBM per device.

```python
import jax
import jax.numpy as jnp
from jax import lax

HEAD_WIDTH = 128
KEY_VALUE_HEADS = 8
QUERY_GROUP = 4
HQ = 32
TOKEN_COUNT = 2048


def draw_pair(key):
    key_offset = jax.random.truncated_normal(jax.random.fold_in(key, 11), -5.0, 5.0, (TOKEN_COUNT, KEY_VALUE_HEADS, HEAD_WIDTH), jnp.float32)
    query_offset = jax.random.truncated_normal(jax.random.fold_in(key, 12), -5.0, 5.0, (TOKEN_COUNT, KEY_VALUE_HEADS, QUERY_GROUP, HEAD_WIDTH), jnp.float32)
    key_row_block = key_offset
    query_row_block = query_offset
    return (query_row_block.reshape(TOKEN_COUNT, KEY_VALUE_HEADS * QUERY_GROUP * HEAD_WIDTH), key_row_block.reshape(TOKEN_COUNT, KEY_VALUE_HEADS * HEAD_WIDTH))


def draw_query(key, part):
    return draw_pair(key)[0].astype(jnp.bfloat16)


def draw_keys(key, part):
    return draw_pair(key)[1].astype(jnp.bfloat16)


def levels(key, dims, pieces, smallest, top_value):
    loudness, own = 1.0, jax.random.fold_in(key, 6)
    for dim, blocks in pieces:
        draws = jnp.exp(jax.random.uniform(jax.random.fold_in(own, dim), (blocks,), jnp.float32, smallest / len(pieces), top_value / len(pieces)))
        loudness = loudness * jnp.repeat(draws, dims[dim] // blocks).reshape([-1 if axis == dim else 1 for axis in range(len(dims))])
    return loudness


def scatter_about(own_key, extent, width, limit, shards=(), held_as=jnp.bfloat16):
    factor_of = levels(own_key, extent, shards, -0.22, 0.18) if shards else 1.0
    drawn = jax.random.normal(own_key, extent, jnp.float32) * width * factor_of
    return jnp.minimum(jnp.maximum(drawn, -limit), limit).astype(held_as)


def setup_inputs(seed: int = 0) -> dict:
    streams_of = jax.random.split(jax.random.key(seed), 5)
    return {
        "query": draw_query(jax.random.fold_in(streams_of[4], 71), 0),
        "keys": draw_keys(jax.random.fold_in(streams_of[4], 71), 0),
        "values": scatter_about(streams_of[2], (TOKEN_COUNT, KEY_VALUE_HEADS * HEAD_WIDTH), 1.0, 6.0, ((0, 32),)),
        "output_gradient": scatter_about(streams_of[3], (TOKEN_COUNT, HQ * HEAD_WIDTH), 1.0, 6.0, ((0, 32),)),
    }


def one_group(group_args):
    group_query, group_keys, group_values, group_grad = group_args
    score_scale = HEAD_WIDTH ** -0.5
    position = jnp.arange(TOKEN_COUNT)
    allowed = position[:, None] >= position[None, :]
    key_sum = jnp.zeros((TOKEN_COUNT, HEAD_WIDTH), jnp.float32)
    value_sum = jnp.zeros((TOKEN_COUNT, HEAD_WIDTH), jnp.float32)
    outputs = []
    query_grads = []
    for head in range(QUERY_GROUP):
        head_query = group_query[:, head]
        head_grad = group_grad[:, head]
        logits = score_scale * jnp.dot(head_query, group_keys.T, preferred_element_type=jnp.float32)
        logits = jnp.where(allowed, logits, -1e30)
        row_max = jnp.max(logits, axis=1, keepdims=True)
        lse = row_max + jnp.log(jnp.sum(jnp.exp(logits - row_max), axis=1, keepdims=True))
        probs = jnp.where(allowed, jnp.exp(logits - lse), 0.0)
        weights = probs.astype(jnp.bfloat16)
        attention = jnp.dot(weights, group_values, preferred_element_type=jnp.float32).astype(jnp.bfloat16)
        row_delta = jnp.sum(head_grad.astype(jnp.float32) * attention.astype(jnp.float32), axis=1, keepdims=True)
        prob_grad = jnp.dot(head_grad, group_values.T, preferred_element_type=jnp.float32)
        score_grad = (probs * (prob_grad - row_delta)).astype(jnp.bfloat16)
        query_grads.append((score_scale * jnp.dot(score_grad, group_keys, preferred_element_type=jnp.float32)).astype(jnp.bfloat16))
        outputs.append(attention)
        key_sum = key_sum + jnp.dot(score_grad.T, head_query, preferred_element_type=jnp.float32)
        value_sum = value_sum + jnp.dot(weights.T, head_grad, preferred_element_type=jnp.float32)
    return (jnp.stack(outputs, axis=1), jnp.stack(query_grads, axis=1),
            (score_scale * key_sum).astype(jnp.bfloat16), value_sum.astype(jnp.bfloat16))


def reference(query, keys, values, output_gradient):
    query_grouped = query.reshape(TOKEN_COUNT, KEY_VALUE_HEADS, QUERY_GROUP, HEAD_WIDTH).transpose(1, 0, 2, 3)
    gradient_grouped = output_gradient.reshape(TOKEN_COUNT, KEY_VALUE_HEADS, QUERY_GROUP, HEAD_WIDTH).transpose(1, 0, 2, 3)
    keys_grouped = keys.reshape(TOKEN_COUNT, KEY_VALUE_HEADS, HEAD_WIDTH).transpose(1, 0, 2)
    values_grouped = values.reshape(TOKEN_COUNT, KEY_VALUE_HEADS, HEAD_WIDTH).transpose(1, 0, 2)
    attention, query_grad, key_gradient_rows, value_gradient_rows = lax.map(one_group, (query_grouped, keys_grouped, values_grouped, gradient_grouped))
    attn_out = attention.transpose(1, 0, 2, 3).reshape(TOKEN_COUNT, HQ * HEAD_WIDTH)
    grad_query = query_grad.transpose(1, 0, 2, 3).reshape(TOKEN_COUNT, HQ * HEAD_WIDTH)
    key_gradient = key_gradient_rows.transpose(1, 0, 2).reshape(TOKEN_COUNT, KEY_VALUE_HEADS * HEAD_WIDTH)
    value_gradient = value_gradient_rows.transpose(1, 0, 2).reshape(TOKEN_COUNT, KEY_VALUE_HEADS * HEAD_WIDTH)
    return (attn_out, grad_query, key_gradient, value_gradient)
```

```python
import functools
import math

import jax
import jax.numpy as jnp
from jax import lax
from jax.experimental import pallas as pl
from jax.experimental.pallas import tpu as pltpu
from jax.sharding import PartitionSpec as P

HEAD_WIDTH = 128
MESH = pl.DeviceIdType.MESH
SCALE = HEAD_WIDTH ** (-0.5)
LOG2_SCALE = SCALE * math.log2(math.e)
MASKED = -1e30


def dot(a, b):
    return jnp.dot(a, b, preferred_element_type=jnp.float32)


def kernel(
    sizes,
    query, keys, values, grads,
    out_ref, dq_ref, dk_ref, dv_ref,
    q_all, g_all, kv_all, o_buf, dq_buf, fin,
    q_rows, q_cols, g_rows, g_cols, k_cols, v_cols,
    row_max, row_sum, lse, delta, acc, dq_acc, pair, part_out, part_in,
    own_sem, in_send, in_recv, kv_send, kv_recv, part_send, part_recv, out_send, out_recv,
):
    tp, inner, planes, tok, group, block = sizes
    peers = tp * inner
    chunk = peers * tok
    splits = chunk // block
    jobs = group * splits
    wide = group * HEAD_WIDTH
    ctx_index = lax.axis_index("ctx")
    tp_index = lax.axis_index("tp")
    plane = ctx_index // inner
    lane = ctx_index % inner
    me = lane * tp + tp_index

    def peer_id(p):
        return (plane * inner + p // tp, p % tp)

    def plane_id(z):
        return (z * inner + lane, tp_index)

    barrier = pltpu.get_barrier_semaphore()

    def greet(d, _):
        pl.semaphore_signal(
            barrier, inc=1, device_id=peer_id((me + d) % peers), device_id_type=MESH
        )
        return 0

    lax.fori_loop(1, peers, greet, 0)

    @pl.when(plane > 0)
    def _():
        pl.semaphore_signal(barrier, inc=1, device_id=plane_id(plane - 1), device_id_type=MESH)

    @pl.when(plane < planes - 1)
    def _():
        pl.semaphore_signal(barrier, inc=1, device_id=plane_id(plane + 1), device_id_type=MESH)

    expected = (
        (peers - 1)
        + jnp.where(plane > 0, 1, 0).astype(jnp.int32)
        + jnp.where(plane < planes - 1, 1, 0).astype(jnp.int32)
    )
    pl.semaphore_wait(barrier, expected)

    def cols(p, width):
        return pl.ds(pl.multiple_of(p * width, HEAD_WIDTH), width)

    def rows(p):
        return pl.ds(pl.multiple_of(p * tok, tok), tok)

    def in_pair(a, src_slot, dst_slot):
        if a == 0:
            return keys.at[:, cols(dst_slot, HEAD_WIDTH)], kv_all.at[plane, 0, rows(src_slot), :]
        if a == 1:
            return values.at[:, cols(dst_slot, HEAD_WIDTH)], kv_all.at[plane, 1, rows(src_slot), :]
        if a == 2:
            return query.at[:, cols(dst_slot, wide)], q_all.at[rows(src_slot), :]
        return grads.at[:, cols(dst_slot, wide)], g_all.at[rows(src_slot), :]

    def in_copy(a, src_slot, dst_slot):
        src, dst = in_pair(a, src_slot, dst_slot)
        return pltpu.make_async_remote_copy(
            src_ref=src, dst_ref=dst,
            send_sem=in_send.at[a, dst_slot], recv_sem=in_recv.at[a, src_slot],
            device_id=peer_id(dst_slot), device_id_type=MESH,
        )

    def own_copy(a):
        src, dst = in_pair(a, me, me)
        return pltpu.make_async_copy(src, dst, own_sem.at[a])

    def send_in(arrays):
        def one(d, _):
            for a in arrays:
                in_copy(a, me, (me + d) % peers).start()
            return 0

        lax.fori_loop(1, peers, one, 0)

    def await_in(arrays):
        for a in arrays:
            own_copy(a).wait()

        def one(d, _):
            for a in arrays:
                in_copy(a, (me + d) % peers, me).wait_recv()
            return 0

        lax.fori_loop(1, peers, one, 0)

    for a in range(4):
        own_copy(a).start()
    send_in((0, 1))
    send_in((2,))
    send_in((3,))

    def kv_copy(j, target):
        return pltpu.make_async_remote_copy(
            src_ref=kv_all.at[j], dst_ref=kv_all.at[j],
            send_sem=kv_send.at[j], recv_sem=kv_recv.at[j],
            device_id=plane_id(target), device_id_type=MESH,
        )

    await_in((0, 1))

    @pl.when(plane < planes - 1)
    def _():
        kv_copy(plane, plane + 1).start()

    def spread(whole, by_rows, by_cols):
        for h in range(group):
            for s in range(splits):
                piece = whole[s * block:(s + 1) * block, h * HEAD_WIDTH:(h + 1) * HEAD_WIDTH]
                by_rows[h * splits + s] = piece
                by_cols[h * splits + s] = piece.T

    await_in((2,))
    spread(q_all, q_rows, q_cols)

    key_pos = lax.broadcasted_iota(jnp.int32, (chunk, block), 0)
    query_pos = lax.broadcasted_iota(jnp.int32, (chunk, block), 1)

    def masked(i, s):
        return jnp.where(key_pos <= query_pos + (i % splits) * block, s, MASKED)

    v_cols[...] = kv_all[plane, 1].T

    def first(i, _):
        s = masked(i, dot(kv_all[plane, 0], q_cols[i]))
        top = jnp.max(s, axis=0, keepdims=True)
        p = jnp.exp2((s - top) * LOG2_SCALE)
        row_max[i] = top
        row_sum[i] = jnp.sum(p, axis=0, keepdims=True)
        acc[i] = dot(v_cols[...], p.astype(jnp.bfloat16))
        return 0

    lax.fori_loop(0, jobs, first, 0)

    def forward(n, _):
        j = plane - 1 - n
        kv_copy(j, plane).wait_recv()

        @pl.when(plane < planes - 1)
        def _():
            kv_copy(j, plane + 1).start()

        v_cols[...] = kv_all[j, 1].T

        def one(i, _):
            s = dot(kv_all[j, 0], q_cols[i])
            old = row_max[i]
            top = jnp.maximum(old, jnp.max(s, axis=0, keepdims=True))
            p = jnp.exp2((s - top) * LOG2_SCALE)
            shrink = jnp.exp2((old - top) * LOG2_SCALE)
            row_max[i] = top
            row_sum[i] = row_sum[i] * shrink + jnp.sum(p, axis=0, keepdims=True)
            acc[i] = acc[i] * shrink + dot(v_cols[...], p.astype(jnp.bfloat16))
            return 0

        lax.fori_loop(0, jobs, one, 0)
        return 0

    lax.fori_loop(0, plane, forward, 0)

    await_in((3,))
    spread(g_all, g_rows, g_cols)

    for h in range(group):
        for s in range(splits):
            i = h * splits + s
            total = row_sum[i]
            rounded = (acc[i] / total).astype(jnp.bfloat16)
            lse[i] = row_max[i] * LOG2_SCALE + jnp.log2(total)
            delta[i] = jnp.sum(
                g_cols[i].astype(jnp.float32) * rounded.astype(jnp.float32), axis=0, keepdims=True
            )
            o_buf[s * block:(s + 1) * block, h * HEAD_WIDTH:(h + 1) * HEAD_WIDTH] = rounded.T

    def out_pair(a, src_slot, dst_slot):
        if a == 0:
            return o_buf.at[rows(dst_slot), :], out_ref.at[:, cols(src_slot, wide)]
        if a == 1:
            return dq_buf.at[rows(dst_slot), :], dq_ref.at[:, cols(src_slot, wide)]
        if a == 2:
            return fin.at[0, rows(dst_slot), :], dk_ref.at[:, cols(src_slot, HEAD_WIDTH)]
        return fin.at[1, rows(dst_slot), :], dv_ref.at[:, cols(src_slot, HEAD_WIDTH)]

    def out_copy(a, src_slot, dst_slot):
        src, dst = out_pair(a, src_slot, dst_slot)
        return pltpu.make_async_remote_copy(
            src_ref=src, dst_ref=dst,
            send_sem=out_send.at[a, dst_slot], recv_sem=out_recv.at[a, src_slot],
            device_id=peer_id(dst_slot), device_id_type=MESH,
        )

    def own_out(a):
        src, dst = out_pair(a, me, me)
        return pltpu.make_async_copy(src, dst, own_sem.at[4 + a])

    def send_out(arrays):
        for a in arrays:
            own_out(a).start()

        def one(d, _):
            for a in arrays:
                out_copy(a, me, (me + d) % peers).start()
            return 0

        lax.fori_loop(1, peers, one, 0)

    send_out((0,))
    dq_acc[...] = jnp.zeros_like(dq_acc)

    def part_copy(j, target):
        return pltpu.make_async_remote_copy(
            src_ref=part_out.at[j], dst_ref=part_in.at[j],
            send_sem=part_send.at[j], recv_sem=part_recv.at[j],
            device_id=plane_id(target), device_id_type=MESH,
        )

    def backward(j, diagonal):
        pair[...] = jnp.zeros_like(pair)
        k_cols[...] = kv_all[j, 0].T

        def one(i, _):
            s = dot(kv_all[j, 0], q_cols[i])
            if diagonal:
                s = masked(i, s)
            p = jnp.exp2(s * LOG2_SCALE - lse[i])
            dp = dot(kv_all[j, 1], g_cols[i])
            ds = (p * (dp - delta[i])).astype(jnp.bfloat16)
            pair[1] += dot(p.astype(jnp.bfloat16), g_rows[i])
            pair[0] += dot(ds, q_rows[i])
            dq_acc[i] += dot(k_cols[...], ds)
            return 0

        lax.fori_loop(0, jobs, one, 0)

        @pl.when(plane < planes - 1)
        def _():
            part_copy(j, plane).wait_recv()
            pair[...] += part_in[j].astype(jnp.float32)

    def earlier(j, _):
        backward(j, False)
        part_out[j] = pair[...].astype(jnp.bfloat16)
        part_copy(j, plane - 1).start()
        return 0

    lax.fori_loop(0, plane, earlier, 0)
    backward(plane, True)
    fin[0] = (pair[0] * SCALE).astype(jnp.bfloat16)
    fin[1] = pair[1].astype(jnp.bfloat16)
    send_out((2, 3))
    for h in range(group):
        for s in range(splits):
            piece = (dq_acc[h * splits + s] * SCALE).astype(jnp.bfloat16)
            dq_buf[s * block:(s + 1) * block, h * HEAD_WIDTH:(h + 1) * HEAD_WIDTH] = piece.T
    send_out((1,))

    def drain(d, _):
        p = (me + d) % peers
        for a in range(4):
            in_copy(a, me, p).wait_send()
            out_copy(a, me, p).wait_send()
            out_copy(a, p, me).wait_recv()
        return 0

    lax.fori_loop(1, peers, drain, 0)
    for a in range(4):
        own_out(a).wait()

    @pl.when(plane < planes - 1)
    def _():
        def one(j, _):
            kv_copy(j, plane + 1).wait_send()
            return 0

        lax.fori_loop(0, plane + 1, one, 0)

    def sent(j, _):
        part_copy(j, plane - 1).wait_send()
        return 0

    lax.fori_loop(0, plane, sent, 0)


def shards(query, keys, values, output_gradient):
    ctx = lax.axis_size("ctx")
    tp = lax.axis_size("tp")
    tok, model = query.shape
    kv_heads = keys.shape[1] // HEAD_WIDTH
    group = model // keys.shape[1]
    inner = kv_heads // tp
    planes = ctx // inner
    peers = kv_heads
    chunk = peers * tok
    block = min(256, chunk)
    jobs = group * (chunk // block)
    wide = group * HEAD_WIDTH
    bf16, f32 = jnp.bfloat16, jnp.float32
    hbm = pl.BlockSpec(memory_space=pl.ANY)
    dma = pltpu.SemaphoreType.DMA
    return pl.pallas_call(
        functools.partial(kernel, (tp, inner, planes, tok, group, block)),
        out_shape=tuple(
            jax.ShapeDtypeStruct(a.shape, a.dtype) for a in (query, query, keys, values)
        ),
        in_specs=[hbm] * 4,
        out_specs=(hbm,) * 4,
        scratch_shapes=[
            pltpu.VMEM((chunk, wide), bf16),
            pltpu.VMEM((chunk, wide), bf16),
            pltpu.VMEM((planes, 2, chunk, HEAD_WIDTH), bf16),
            pltpu.VMEM((chunk, wide), bf16),
            pltpu.VMEM((chunk, wide), bf16),
            pltpu.VMEM((2, chunk, HEAD_WIDTH), bf16),
            pltpu.VMEM((jobs, block, HEAD_WIDTH), bf16),
            pltpu.VMEM((jobs, HEAD_WIDTH, block), bf16),
            pltpu.VMEM((jobs, block, HEAD_WIDTH), bf16),
            pltpu.VMEM((jobs, HEAD_WIDTH, block), bf16),
            pltpu.VMEM((HEAD_WIDTH, chunk), bf16),
            pltpu.VMEM((HEAD_WIDTH, chunk), bf16),
            pltpu.VMEM((jobs, 1, block), f32),
            pltpu.VMEM((jobs, 1, block), f32),
            pltpu.VMEM((jobs, 1, block), f32),
            pltpu.VMEM((jobs, 1, block), f32),
            pltpu.VMEM((jobs, HEAD_WIDTH, block), f32),
            pltpu.VMEM((jobs, HEAD_WIDTH, block), f32),
            pltpu.VMEM((2, chunk, HEAD_WIDTH), f32),
            pltpu.VMEM((planes, 2, chunk, HEAD_WIDTH), bf16),
            pltpu.VMEM((planes, 2, chunk, HEAD_WIDTH), bf16),
            dma((8,)),
            dma((4, peers)),
            dma((4, peers)),
            dma((planes,)),
            dma((planes,)),
            dma((planes,)),
            dma((planes,)),
            dma((4, peers)),
            dma((4, peers)),
        ],
        compiler_params=pltpu.CompilerParams(
            collective_id=0, has_side_effects=True, vmem_limit_bytes=48 * 1024 * 1024
        ),
    )(query, keys, values, output_gradient)


def solution(mesh):
    placed = (P(("ctx", "tp"), None),) * 4
    return jax.shard_map(
        shards, mesh=mesh, in_specs=placed, out_specs=placed, check_vma=False
    )
```

```python
import functools
import math

import jax
import jax.numpy as jnp
from jax import lax
from jax.experimental import pallas as pl
from jax.experimental.pallas import tpu as pltpu
from jax.sharding import PartitionSpec as P

HEAD_WIDTH = 128
MESH = pl.DeviceIdType.MESH
SCALE = HEAD_WIDTH ** (-0.5)
LOG2_SCALE = SCALE * math.log2(math.e)
MASKED = -1e30


def dot(a, b):
    return jnp.dot(a, b, preferred_element_type=jnp.float32)


def kernel(
    sizes,
    query, keys, values, grads,
    out_ref, dq_ref, dk_ref, dv_ref,
    q_all, g_all, kv_all, o_buf, dq_buf, fin,
    q_rows, q_cols, g_rows, g_cols, k_cols, v_cols,
    row_max, row_sum, lse, delta, acc, o_cols, dq_acc, pair, part_out, part_in,
    own_sem, in_send, in_recv, kv_send, kv_recv, part_send, part_recv, out_send, out_recv,
):
    tp, inner, planes, tok, group, block = sizes
    peers = tp * inner
    chunk = peers * tok
    splits = chunk // block
    jobs = group * splits
    wide = group * HEAD_WIDTH
    ctx_index = lax.axis_index("ctx")
    tp_index = lax.axis_index("tp")
    plane = ctx_index // inner
    lane = ctx_index % inner
    me = lane * tp + tp_index

    def peer_id(p):
        return (plane * inner + p // tp, p % tp)

    def plane_id(z):
        return (z * inner + lane, tp_index)

    barrier = pltpu.get_barrier_semaphore()

    def greet(d, _):
        pl.semaphore_signal(
            barrier, inc=1, device_id=peer_id((me + d) % peers), device_id_type=MESH
        )
        return 0

    lax.fori_loop(1, peers, greet, 0)

    @pl.when(plane > 0)
    def _():
        pl.semaphore_signal(barrier, inc=1, device_id=plane_id(plane - 1), device_id_type=MESH)

    @pl.when(plane < planes - 1)
    def _():
        pl.semaphore_signal(barrier, inc=1, device_id=plane_id(plane + 1), device_id_type=MESH)

    expected = (
        (peers - 1)
        + jnp.where(plane > 0, 1, 0).astype(jnp.int32)
        + jnp.where(plane < planes - 1, 1, 0).astype(jnp.int32)
    )
    pl.semaphore_wait(barrier, expected)

    def cols(p, width):
        return pl.ds(pl.multiple_of(p * width, HEAD_WIDTH), width)

    def rows(p):
        return pl.ds(pl.multiple_of(p * tok, tok), tok)

    def in_pair(a, src_slot, dst_slot):
        if a == 0:
            return keys.at[:, cols(dst_slot, HEAD_WIDTH)], kv_all.at[plane, 0, rows(src_slot), :]
        if a == 1:
            return values.at[:, cols(dst_slot, HEAD_WIDTH)], kv_all.at[plane, 1, rows(src_slot), :]
        if a == 2:
            return query.at[:, cols(dst_slot, wide)], q_all.at[rows(src_slot), :]
        return grads.at[:, cols(dst_slot, wide)], g_all.at[rows(src_slot), :]

    def in_copy(a, src_slot, dst_slot):
        src, dst = in_pair(a, src_slot, dst_slot)
        return pltpu.make_async_remote_copy(
            src_ref=src, dst_ref=dst,
            send_sem=in_send.at[a, dst_slot], recv_sem=in_recv.at[a, src_slot],
            device_id=peer_id(dst_slot), device_id_type=MESH,
        )

    def own_copy(a):
        src, dst = in_pair(a, me, me)
        return pltpu.make_async_copy(src, dst, own_sem.at[a])

    def send_in(arrays):
        def one(d, _):
            for a in arrays:
                in_copy(a, me, (me + d) % peers).start()
            return 0

        lax.fori_loop(1, peers, one, 0)

    def await_in(arrays):
        for a in arrays:
            own_copy(a).wait()

        def one(d, _):
            for a in arrays:
                in_copy(a, (me + d) % peers, me).wait_recv()
            return 0

        lax.fori_loop(1, peers, one, 0)

    for a in range(4):
        own_copy(a).start()
    send_in((0, 1))
    send_in((2,))
    send_in((3,))

    def kv_copy(j, target):
        return pltpu.make_async_remote_copy(
            src_ref=kv_all.at[j], dst_ref=kv_all.at[j],
            send_sem=kv_send.at[j], recv_sem=kv_recv.at[j],
            device_id=plane_id(target), device_id_type=MESH,
        )

    await_in((0, 1))
    top_plane = plane == planes - 1

    @pl.when(plane < planes - 1)
    def _():
        kv_copy(plane, plane + 1).start()

        def relay(n, _):
            j = plane - 1 - n
            kv_copy(j, plane).wait_recv()
            kv_copy(j, plane + 1).start()
            return 0

        lax.fori_loop(0, plane, relay, 0)

    def spread(whole, by_rows, by_cols):
        for h in range(group):
            for s in range(splits):
                piece = whole[s * block:(s + 1) * block, h * HEAD_WIDTH:(h + 1) * HEAD_WIDTH]
                by_rows[h * splits + s] = piece
                by_cols[h * splits + s] = piece.T

    await_in((2,))
    spread(q_all, q_rows, q_cols)

    def masked(s, split):
        shape = s.shape
        key_pos = lax.broadcasted_iota(jnp.int32, shape, 0)
        query_pos = lax.broadcasted_iota(jnp.int32, shape, 1) + split * block
        return jnp.where(key_pos <= query_pos, s, MASKED)

    v_cols[...] = kv_all[plane, 1].T

    def first(h, _):
        for split in range(splits):
            i, seen = h * splits + split, (split + 1) * block
            s = masked(dot(kv_all[plane, 0, :seen], q_cols[i]), split)
            top = jnp.max(s, axis=0, keepdims=True)
            p = jnp.exp2((s - top) * LOG2_SCALE)
            row_max[i] = top
            row_sum[i] = jnp.sum(p, axis=0, keepdims=True)
            acc[i] = dot(v_cols[:, :seen], p.astype(jnp.bfloat16))
        return 0

    lax.fori_loop(0, group, first, 0)

    def take_grads():
        await_in((3,))
        spread(g_all, g_rows, g_cols)

    @pl.when(plane == 0)
    def _():
        take_grads()

    def forward(n, _):
        j = plane - 1 - n

        @pl.when(j == 0)
        def _():
            take_grads()

        @pl.when(top_plane)
        def _():
            kv_copy(j, plane).wait_recv()

        v_cols[...] = kv_all[j, 1].T

        def one(i, _):
            s = dot(kv_all[j, 0], q_cols[i])
            old = row_max[i]
            top = jnp.maximum(old, jnp.max(s, axis=0, keepdims=True))
            p = jnp.exp2((s - top) * LOG2_SCALE)
            shrink = jnp.exp2((old - top) * LOG2_SCALE)
            row_max[i] = top
            row_sum[i] = row_sum[i] * shrink + jnp.sum(p, axis=0, keepdims=True)
            acc[i] = acc[i] * shrink + dot(v_cols[...], p.astype(jnp.bfloat16))
            return 0

        lax.fori_loop(0, jobs, one, 0)
        return 0

    lax.fori_loop(0, plane, forward, 0)

    for i in range(jobs):
        total = row_sum[i]
        rounded = (acc[i] / total).astype(jnp.bfloat16)
        o_cols[i] = rounded
        lse[i] = row_max[i] * LOG2_SCALE + jnp.log2(total)
        delta[i] = jnp.sum(
            g_cols[i].astype(jnp.float32) * rounded.astype(jnp.float32), axis=0, keepdims=True
        )

    def out_pair(a, src_slot, dst_slot):
        if a == 0:
            return o_buf.at[rows(dst_slot), :], out_ref.at[:, cols(src_slot, wide)]
        if a == 1:
            return dq_buf.at[rows(dst_slot), :], dq_ref.at[:, cols(src_slot, wide)]
        if a == 2:
            return fin.at[0, rows(dst_slot), :], dk_ref.at[:, cols(src_slot, HEAD_WIDTH)]
        return fin.at[1, rows(dst_slot), :], dv_ref.at[:, cols(src_slot, HEAD_WIDTH)]

    def out_copy(a, src_slot, dst_slot):
        src, dst = out_pair(a, src_slot, dst_slot)
        return pltpu.make_async_remote_copy(
            src_ref=src, dst_ref=dst,
            send_sem=out_send.at[a, dst_slot], recv_sem=out_recv.at[a, src_slot],
            device_id=peer_id(dst_slot), device_id_type=MESH,
        )

    def own_out(a):
        src, dst = out_pair(a, me, me)
        return pltpu.make_async_copy(src, dst, own_sem.at[4 + a])

    def send_out(arrays):
        for a in arrays:
            own_out(a).start()

        def one(d, _):
            for a in arrays:
                out_copy(a, me, (me + d) % peers).start()
            return 0

        lax.fori_loop(1, peers, one, 0)

    dq_acc[...] = jnp.zeros_like(dq_acc)

    def part_copy(j, target):
        return pltpu.make_async_remote_copy(
            src_ref=part_out.at[j], dst_ref=part_in.at[j],
            send_sem=part_send.at[j], recv_sem=part_recv.at[j],
            device_id=plane_id(target), device_id_type=MESH,
        )

    def gradients(j, i, seen, split):
        s = dot(kv_all[j, 0, :seen], q_cols[i])
        if split is not None:
            s = masked(s, split)
        p = jnp.exp2(s * LOG2_SCALE - lse[i])
        dp = dot(kv_all[j, 1, :seen], g_cols[i])
        ds = (p * (dp - delta[i])).astype(jnp.bfloat16)
        pair[j, 1, :seen] += dot(p.astype(jnp.bfloat16), g_rows[i])
        pair[j, 0, :seen] += dot(ds, q_rows[i])
        dq_acc[i] += dot(k_cols[:, :seen], ds)

    def backward(j, diagonal):
        pair[j] = jnp.zeros(pair.shape[1:], jnp.float32)
        k_cols[...] = kv_all[j, 0].T

        def one(i, _):
            gradients(j, i, chunk, None)
            return 0

        def triangle(h, _):
            for split in range(splits):
                gradients(j, h * splits + split, (split + 1) * block, split)
            return 0

        if diagonal:
            lax.fori_loop(0, group, triangle, 0)
        else:
            lax.fori_loop(0, jobs, one, 0)

    def earlier(j, _):
        backward(j, False)

        @pl.when(top_plane)
        def _():
            part_out[j] = pair[j].astype(jnp.bfloat16)
            part_copy(j, plane - 1).start()

        return 0

    lax.fori_loop(0, plane, earlier, 0)

    def gather_cols(pieces, dst, factor):
        for h in range(group):
            for s in range(splits):
                piece = pieces[h * splits + s]
                if factor is not None:
                    piece = (piece * factor).astype(jnp.bfloat16)
                dst[s * block:(s + 1) * block, h * HEAD_WIDTH:(h + 1) * HEAD_WIDTH] = piece.T

    gather_cols(o_cols, o_buf, None)
    send_out((0,))
    backward(plane, True)
    gather_cols(dq_acc, dq_buf, SCALE)
    send_out((1,))

    @pl.when(plane < planes - 1)
    def _():
        def chain(j, _):
            part_copy(j, plane).wait_recv()
            part_out[j] = (pair[j] + part_in[j].astype(jnp.float32)).astype(jnp.bfloat16)
            part_copy(j, plane - 1).start()
            return 0

        lax.fori_loop(0, plane, chain, 0)
        part_copy(plane, plane).wait_recv()
        pair[plane] += part_in[plane].astype(jnp.float32)

    fin[0] = (pair[plane, 0] * SCALE).astype(jnp.bfloat16)
    fin[1] = pair[plane, 1].astype(jnp.bfloat16)
    send_out((2, 3))

    def drain(d, _):
        p = (me + d) % peers
        for a in range(4):
            in_copy(a, me, p).wait_send()
            out_copy(a, me, p).wait_send()
            out_copy(a, p, me).wait_recv()
        return 0

    lax.fori_loop(1, peers, drain, 0)
    for a in range(4):
        own_out(a).wait()

    @pl.when(plane < planes - 1)
    def _():
        def one(j, _):
            kv_copy(j, plane + 1).wait_send()
            return 0

        lax.fori_loop(0, plane + 1, one, 0)

    def sent(j, _):
        part_copy(j, plane - 1).wait_send()
        return 0

    lax.fori_loop(0, plane, sent, 0)


def shards(query, keys, values, output_gradient):
    ctx = lax.axis_size("ctx")
    tp = lax.axis_size("tp")
    tok, model = query.shape
    kv_heads = keys.shape[1] // HEAD_WIDTH
    group = model // keys.shape[1]
    inner = kv_heads // tp
    planes = ctx // inner
    peers = kv_heads
    chunk = peers * tok
    block = min(256, chunk)
    jobs = group * (chunk // block)
    wide = group * HEAD_WIDTH
    bf16, f32 = jnp.bfloat16, jnp.float32
    hbm = pl.BlockSpec(memory_space=pl.ANY)
    dma = pltpu.SemaphoreType.DMA
    return pl.pallas_call(
        functools.partial(kernel, (tp, inner, planes, tok, group, block)),
        out_shape=tuple(
            jax.ShapeDtypeStruct(a.shape, a.dtype) for a in (query, query, keys, values)
        ),
        in_specs=[hbm] * 4,
        out_specs=(hbm,) * 4,
        scratch_shapes=[
            pltpu.VMEM((chunk, wide), bf16),
            pltpu.VMEM((chunk, wide), bf16),
            pltpu.VMEM((planes, 2, chunk, HEAD_WIDTH), bf16),
            pltpu.VMEM((chunk, wide), bf16),
            pltpu.VMEM((chunk, wide), bf16),
            pltpu.VMEM((2, chunk, HEAD_WIDTH), bf16),
            pltpu.VMEM((jobs, block, HEAD_WIDTH), bf16),
            pltpu.VMEM((jobs, HEAD_WIDTH, block), bf16),
            pltpu.VMEM((jobs, block, HEAD_WIDTH), bf16),
            pltpu.VMEM((jobs, HEAD_WIDTH, block), bf16),
            pltpu.VMEM((HEAD_WIDTH, chunk), bf16),
            pltpu.VMEM((HEAD_WIDTH, chunk), bf16),
            pltpu.VMEM((jobs, 1, block), f32),
            pltpu.VMEM((jobs, 1, block), f32),
            pltpu.VMEM((jobs, 1, block), f32),
            pltpu.VMEM((jobs, 1, block), f32),
            pltpu.VMEM((jobs, HEAD_WIDTH, block), f32),
            pltpu.VMEM((jobs, HEAD_WIDTH, block), bf16),
            pltpu.VMEM((jobs, HEAD_WIDTH, block), f32),
            pltpu.VMEM((planes, 2, chunk, HEAD_WIDTH), f32),
            pltpu.VMEM((planes, 2, chunk, HEAD_WIDTH), bf16),
            pltpu.VMEM((planes, 2, chunk, HEAD_WIDTH), bf16),
            dma((8,)),
            dma((4, peers)),
            dma((4, peers)),
            dma((planes,)),
            dma((planes,)),
            dma((planes,)),
            dma((planes,)),
            dma((4, peers)),
            dma((4, peers)),
        ],
        compiler_params=pltpu.CompilerParams(
            collective_id=0, has_side_effects=True, vmem_limit_bytes=60 * 1024 * 1024
        ),
    )(query, keys, values, output_gradient)


def solution(mesh):
    placed = (P(("ctx", "tp"), None),) * 4
    return jax.shard_map(
        shards, mesh=mesh, in_specs=placed, out_specs=placed, check_vma=False
    )
```

```python
import functools
import math

import jax
import jax.numpy as jnp
from jax import lax
from jax.experimental import pallas as pl
from jax.experimental.pallas import tpu as pltpu
from jax.sharding import PartitionSpec as P

HEAD_WIDTH = 128
MESH = pl.DeviceIdType.MESH
SCALE = HEAD_WIDTH ** (-0.5)
LOG2_SCALE = SCALE * math.log2(math.e)
MASKED = -1e30


def dot(a, b):
    return jnp.dot(a, b, preferred_element_type=jnp.float32)


def kernel(
    sizes,
    query, keys, values, grads,
    out_ref, dq_ref, dk_ref, dv_ref,
    q_all, g_all, kv_all, o_buf, dq_buf, fin,
    q_rows, q_cols, g_rows, g_cols, k_cols, v_cols,
    row_max, row_sum, lse, delta, acc, o_cols, dq_acc, p_all, ds_all, pair, part_out, part_in,
    own_sem, in_send, in_recv, kv_send, kv_recv, part_send, part_recv, out_send, out_recv,
):
    tp, inner, planes, tok, group, block = sizes
    peers = tp * inner
    chunk = peers * tok
    splits = chunk // block
    jobs = group * splits
    wide = group * HEAD_WIDTH
    ctx_index = lax.axis_index("ctx")
    tp_index = lax.axis_index("tp")
    plane = ctx_index // inner
    lane = ctx_index % inner
    me = lane * tp + tp_index

    def peer_id(p):
        return (plane * inner + p // tp, p % tp)

    def plane_id(z):
        return (z * inner + lane, tp_index)

    barrier = pltpu.get_barrier_semaphore()

    def greet(d, _):
        pl.semaphore_signal(
            barrier, inc=1, device_id=peer_id((me + d) % peers), device_id_type=MESH
        )
        return 0

    lax.fori_loop(1, peers, greet, 0)

    @pl.when(plane > 0)
    def _():
        pl.semaphore_signal(barrier, inc=1, device_id=plane_id(plane - 1), device_id_type=MESH)

    @pl.when(plane < planes - 1)
    def _():
        pl.semaphore_signal(barrier, inc=1, device_id=plane_id(plane + 1), device_id_type=MESH)

    expected = (
        (peers - 1)
        + jnp.where(plane > 0, 1, 0).astype(jnp.int32)
        + jnp.where(plane < planes - 1, 1, 0).astype(jnp.int32)
    )
    pl.semaphore_wait(barrier, expected)

    def cols(p, width):
        return pl.ds(pl.multiple_of(p * width, HEAD_WIDTH), width)

    def rows(p):
        return pl.ds(pl.multiple_of(p * tok, tok), tok)

    def in_pair(a, src_slot, dst_slot):
        if a == 0:
            return keys.at[:, cols(dst_slot, HEAD_WIDTH)], kv_all.at[plane, 0, rows(src_slot), :]
        if a == 1:
            return values.at[:, cols(dst_slot, HEAD_WIDTH)], kv_all.at[plane, 1, rows(src_slot), :]
        if a == 2:
            return query.at[:, cols(dst_slot, wide)], q_all.at[rows(src_slot), :]
        return grads.at[:, cols(dst_slot, wide)], g_all.at[rows(src_slot), :]

    def in_copy(a, src_slot, dst_slot):
        src, dst = in_pair(a, src_slot, dst_slot)
        return pltpu.make_async_remote_copy(
            src_ref=src, dst_ref=dst,
            send_sem=in_send.at[a, dst_slot], recv_sem=in_recv.at[a, src_slot],
            device_id=peer_id(dst_slot), device_id_type=MESH,
        )

    def own_copy(a):
        src, dst = in_pair(a, me, me)
        return pltpu.make_async_copy(src, dst, own_sem.at[a])

    def send_in(arrays):
        def one(d, _):
            for a in arrays:
                in_copy(a, me, (me + d) % peers).start()
            return 0

        lax.fori_loop(1, peers, one, 0)

    def await_in(arrays):
        for a in arrays:
            own_copy(a).wait()

        def one(d, _):
            for a in arrays:
                in_copy(a, (me + d) % peers, me).wait_recv()
            return 0

        lax.fori_loop(1, peers, one, 0)

    for a in range(4):
        own_copy(a).start()
    send_in((0, 1))
    send_in((2,))
    send_in((3,))

    def kv_copy(j, target):
        return pltpu.make_async_remote_copy(
            src_ref=kv_all.at[j], dst_ref=kv_all.at[j],
            send_sem=kv_send.at[j], recv_sem=kv_recv.at[j],
            device_id=plane_id(target), device_id_type=MESH,
        )

    await_in((0, 1))
    top_plane = plane == planes - 1

    @pl.when(plane < planes - 1)
    def _():
        kv_copy(plane, plane + 1).start()

        def relay(n, _):
            j = plane - 1 - n
            kv_copy(j, plane).wait_recv()
            kv_copy(j, plane + 1).start()
            return 0

        lax.fori_loop(0, plane, relay, 0)

    def spread(whole, by_rows, by_cols):
        for h in range(group):
            for s in range(splits):
                piece = whole[s * block:(s + 1) * block, h * HEAD_WIDTH:(h + 1) * HEAD_WIDTH]
                by_rows[(h * splits + s) * block:(h * splits + s + 1) * block] = piece
                by_cols[h * splits + s] = piece.T

    await_in((2,))
    spread(q_all, q_rows, q_cols)

    def masked(s, split):
        shape = s.shape
        key_pos = lax.broadcasted_iota(jnp.int32, shape, 0)
        query_pos = lax.broadcasted_iota(jnp.int32, shape, 1) + split * block
        return jnp.where(key_pos <= query_pos, s, MASKED)

    v_cols[...] = kv_all[plane, 1].T

    def first(h, _):
        for split in range(splits):
            i, seen = h * splits + split, (split + 1) * block
            s = masked(dot(kv_all[plane, 0, :seen], q_cols[i]), split)
            top = jnp.max(s, axis=0, keepdims=True)
            p = jnp.exp2((s - top) * LOG2_SCALE)
            row_max[i] = top
            row_sum[i] = jnp.sum(p, axis=0, keepdims=True)
            acc[i] = dot(v_cols[:, :seen], p.astype(jnp.bfloat16))
        return 0

    lax.fori_loop(0, group, first, 0, unroll=2)

    def take_grads():
        await_in((3,))
        spread(g_all, g_rows, g_cols)

    @pl.when(plane == 0)
    def _():
        take_grads()

    def forward(n, _):
        j = plane - 1 - n

        @pl.when(j == 0)
        def _():
            take_grads()

        @pl.when(top_plane)
        def _():
            kv_copy(j, plane).wait_recv()

        v_cols[...] = kv_all[j, 1].T

        def one(i, _):
            s = dot(kv_all[j, 0], q_cols[i])
            old = row_max[i]
            top = jnp.maximum(old, jnp.max(s, axis=0, keepdims=True))
            p = jnp.exp2((s - top) * LOG2_SCALE)
            shrink = jnp.exp2((old - top) * LOG2_SCALE)
            row_max[i] = top
            row_sum[i] = row_sum[i] * shrink + jnp.sum(p, axis=0, keepdims=True)
            acc[i] = acc[i] * shrink + dot(v_cols[...], p.astype(jnp.bfloat16))
            return 0

        lax.fori_loop(0, jobs, one, 0, unroll=4)
        return 0

    lax.fori_loop(0, plane, forward, 0)

    for i in range(jobs):
        total = row_sum[i]
        rounded = (acc[i] / total).astype(jnp.bfloat16)
        o_cols[i] = rounded
        lse[i] = row_max[i] * LOG2_SCALE + jnp.log2(total)
        delta[i] = jnp.sum(
            g_cols[i].astype(jnp.float32) * rounded.astype(jnp.float32), axis=0, keepdims=True
        )

    def out_pair(a, src_slot, dst_slot):
        if a == 0:
            return o_buf.at[rows(dst_slot), :], out_ref.at[:, cols(src_slot, wide)]
        if a == 1:
            return dq_buf.at[rows(dst_slot), :], dq_ref.at[:, cols(src_slot, wide)]
        if a == 2:
            return fin.at[0, rows(dst_slot), :], dk_ref.at[:, cols(src_slot, HEAD_WIDTH)]
        return fin.at[1, rows(dst_slot), :], dv_ref.at[:, cols(src_slot, HEAD_WIDTH)]

    def out_copy(a, src_slot, dst_slot):
        src, dst = out_pair(a, src_slot, dst_slot)
        return pltpu.make_async_remote_copy(
            src_ref=src, dst_ref=dst,
            send_sem=out_send.at[a, dst_slot], recv_sem=out_recv.at[a, src_slot],
            device_id=peer_id(dst_slot), device_id_type=MESH,
        )

    def own_out(a):
        src, dst = out_pair(a, me, me)
        return pltpu.make_async_copy(src, dst, own_sem.at[4 + a])

    def send_out(arrays):
        for a in arrays:
            own_out(a).start()

        def one(d, _):
            for a in arrays:
                out_copy(a, me, (me + d) % peers).start()
            return 0

        lax.fori_loop(1, peers, one, 0)

    dq_acc[...] = jnp.zeros_like(dq_acc)

    def part_copy(j, target):
        return pltpu.make_async_remote_copy(
            src_ref=part_out.at[j], dst_ref=part_in.at[j],
            send_sem=part_send.at[j], recv_sem=part_recv.at[j],
            device_id=plane_id(target), device_id_type=MESH,
        )

    def gradients(j, i, seen, split):
        where = pl.ds(i * block if isinstance(i, int) else pl.multiple_of(i * block, block), block)
        s = dot(kv_all[j, 0, :seen], q_cols[i])
        if split is not None:
            s = masked(s, split)
        p = jnp.exp2(s * LOG2_SCALE - lse[i])
        dp = dot(kv_all[j, 1, :seen], g_cols[i])
        ds = (p * (dp - delta[i])).astype(jnp.bfloat16)
        p_all[:seen, where] = p.astype(jnp.bfloat16)
        ds_all[:seen, where] = ds
        if seen < chunk:
            unseen = jnp.zeros((chunk - seen, block), jnp.bfloat16)
            p_all[seen:, where] = unseen
            ds_all[seen:, where] = unseen
        dq_acc[i] += dot(k_cols[:, :seen], ds)

    def backward(j, diagonal):
        k_cols[...] = kv_all[j, 0].T

        def one(i, _):
            gradients(j, i, chunk, None)
            return 0

        def triangle(h, _):
            for split in range(splits):
                gradients(j, h * splits + split, (split + 1) * block, split)
            return 0

        if diagonal:
            lax.fori_loop(0, group, triangle, 0, unroll=2)
        else:
            lax.fori_loop(0, jobs, one, 0, unroll=4)
        pair[j, 1] = dot(p_all[...], g_rows[...])
        pair[j, 0] = dot(ds_all[...], q_rows[...])

    def earlier(j, _):
        backward(j, False)

        @pl.when(top_plane)
        def _():
            part_out[j] = pair[j].astype(jnp.bfloat16)
            part_copy(j, plane - 1).start()

        return 0

    lax.fori_loop(0, plane, earlier, 0)

    def gather_cols(pieces, dst, factor):
        for h in range(group):
            for s in range(splits):
                piece = pieces[h * splits + s]
                if factor is not None:
                    piece = (piece * factor).astype(jnp.bfloat16)
                dst[s * block:(s + 1) * block, h * HEAD_WIDTH:(h + 1) * HEAD_WIDTH] = piece.T

    gather_cols(o_cols, o_buf, None)
    send_out((0,))
    backward(plane, True)
    gather_cols(dq_acc, dq_buf, SCALE)
    send_out((1,))

    @pl.when(plane < planes - 1)
    def _():
        def chain(j, _):
            part_copy(j, plane).wait_recv()
            part_out[j] = (pair[j] + part_in[j].astype(jnp.float32)).astype(jnp.bfloat16)
            part_copy(j, plane - 1).start()
            return 0

        lax.fori_loop(0, plane, chain, 0)
        part_copy(plane, plane).wait_recv()
        pair[plane] += part_in[plane].astype(jnp.float32)

    fin[0] = (pair[plane, 0] * SCALE).astype(jnp.bfloat16)
    fin[1] = pair[plane, 1].astype(jnp.bfloat16)
    send_out((2, 3))

    def drain(d, _):
        p = (me + d) % peers
        for a in range(4):
            in_copy(a, me, p).wait_send()
            out_copy(a, me, p).wait_send()
            out_copy(a, p, me).wait_recv()
        return 0

    lax.fori_loop(1, peers, drain, 0)
    for a in range(4):
        own_out(a).wait()

    @pl.when(plane < planes - 1)
    def _():
        def one(j, _):
            kv_copy(j, plane + 1).wait_send()
            return 0

        lax.fori_loop(0, plane + 1, one, 0)

    def sent(j, _):
        part_copy(j, plane - 1).wait_send()
        return 0

    lax.fori_loop(0, plane, sent, 0)


def hand_over(*refs):
    sem = refs[8]
    copies = [pltpu.make_async_copy(refs[i], refs[4 + i], sem.at[i]) for i in range(4)]
    for copy in copies:
        copy.start()
    for copy in copies:
        copy.wait()


def shards(query, keys, values, output_gradient):
    ctx = lax.axis_size("ctx")
    tp = lax.axis_size("tp")
    tok, model = query.shape
    kv_heads = keys.shape[1] // HEAD_WIDTH
    group = model // keys.shape[1]
    inner = kv_heads // tp
    planes = ctx // inner
    peers = kv_heads
    chunk = peers * tok
    block = min(256, chunk)
    jobs = group * (chunk // block)
    wide = group * HEAD_WIDTH
    bf16, f32 = jnp.bfloat16, jnp.float32
    anywhere = pl.BlockSpec(memory_space=pl.ANY)
    dma = pltpu.SemaphoreType.DMA
    results = pl.pallas_call(
        functools.partial(kernel, (tp, inner, planes, tok, group, block)),
        out_shape=tuple(
            jax.ShapeDtypeStruct(a.shape, a.dtype) for a in (query, query, keys, values)
        ),
        in_specs=[anywhere] * 4,
        out_specs=(anywhere,) * 4,
        scratch_shapes=[
            pltpu.VMEM((chunk, wide), bf16),
            pltpu.VMEM((chunk, wide), bf16),
            pltpu.VMEM((planes, 2, chunk, HEAD_WIDTH), bf16),
            pltpu.VMEM((chunk, wide), bf16),
            pltpu.VMEM((chunk, wide), bf16),
            pltpu.VMEM((2, chunk, HEAD_WIDTH), bf16),
            pltpu.VMEM((jobs * block, HEAD_WIDTH), bf16),
            pltpu.VMEM((jobs, HEAD_WIDTH, block), bf16),
            pltpu.VMEM((jobs * block, HEAD_WIDTH), bf16),
            pltpu.VMEM((jobs, HEAD_WIDTH, block), bf16),
            pltpu.VMEM((HEAD_WIDTH, chunk), bf16),
            pltpu.VMEM((HEAD_WIDTH, chunk), bf16),
            pltpu.VMEM((jobs, 1, block), f32),
            pltpu.VMEM((jobs, 1, block), f32),
            pltpu.VMEM((jobs, 1, block), f32),
            pltpu.VMEM((jobs, 1, block), f32),
            pltpu.VMEM((jobs, HEAD_WIDTH, block), f32),
            pltpu.VMEM((jobs, HEAD_WIDTH, block), bf16),
            pltpu.VMEM((jobs, HEAD_WIDTH, block), f32),
            pltpu.VMEM((chunk, jobs * block), bf16),
            pltpu.VMEM((chunk, jobs * block), bf16),
            pltpu.VMEM((planes, 2, chunk, HEAD_WIDTH), f32),
            pltpu.VMEM((planes, 2, chunk, HEAD_WIDTH), bf16),
            pltpu.VMEM((planes, 2, chunk, HEAD_WIDTH), bf16),
            dma((8,)),
            dma((4, peers)),
            dma((4, peers)),
            dma((planes,)),
            dma((planes,)),
            dma((planes,)),
            dma((planes,)),
            dma((4, peers)),
            dma((4, peers)),
        ],
        compiler_params=pltpu.CompilerParams(
            collective_id=0, has_side_effects=True, vmem_limit_bytes=64 * 1024 * 1024
        ),
    )(query, keys, values, output_gradient)
    return pl.pallas_call(
        hand_over,
        out_shape=tuple(jax.ShapeDtypeStruct(a.shape, a.dtype) for a in results),
        in_specs=[anywhere] * 4,
        out_specs=(anywhere,) * 4,
        scratch_shapes=[dma((4,))],
        compiler_params=pltpu.CompilerParams(vmem_limit_bytes=64 * 1024 * 1024),
    )(*results)


def solution(mesh):
    placed = (P(("ctx", "tp"), None),) * 4
    return jax.shard_map(
        shards, mesh=mesh, in_specs=placed, out_specs=placed, check_vma=False
    )
```

```python
import functools
import math

import jax
import jax.numpy as jnp
from jax import lax
from jax.experimental import pallas as pl
from jax.experimental.pallas import tpu as pltpu
from jax.sharding import PartitionSpec as P

HEAD_WIDTH = 128
MESH = pl.DeviceIdType.MESH
SCALE = HEAD_WIDTH ** (-0.5)
LOG2_SCALE = SCALE * math.log2(math.e)
MASKED = -1e30


def dot(a, b):
    return jnp.dot(a, b, preferred_element_type=jnp.float32)


def kernel(
    sizes,
    query, keys, values, grads,
    out_ref, dq_ref, dk_ref, dv_ref,
    q_all, g_all, kv_all, o_buf, dq_buf, fin,
    q_rows, q_cols, g_rows, g_cols, k_cols, v_cols,
    row_max, row_sum, lse, delta, acc, o_cols, dq_acc, p_all, ds_all, pair, part_out, part_in,
    own_sem, in_send, in_recv, kv_send, kv_recv, part_send, part_recv, out_send, out_recv,
):
    tp, inner, planes, tok, group, block = sizes
    peers = tp * inner
    chunk = peers * tok
    splits = chunk // block
    jobs = group * splits
    wide = group * HEAD_WIDTH
    ctx_index = lax.axis_index("ctx")
    tp_index = lax.axis_index("tp")
    plane = ctx_index // inner
    lane = ctx_index % inner
    me = lane * tp + tp_index

    def peer_id(p):
        return (plane * inner + p // tp, p % tp)

    def plane_id(z):
        return (z * inner + lane, tp_index)

    barrier = pltpu.get_barrier_semaphore()

    def greet(d, _):
        pl.semaphore_signal(
            barrier, inc=1, device_id=peer_id((me + d) % peers), device_id_type=MESH
        )
        return 0

    lax.fori_loop(1, peers, greet, 0)

    @pl.when(plane > 0)
    def _():
        pl.semaphore_signal(barrier, inc=1, device_id=plane_id(plane - 1), device_id_type=MESH)

    @pl.when(plane < planes - 1)
    def _():
        pl.semaphore_signal(barrier, inc=1, device_id=plane_id(plane + 1), device_id_type=MESH)

    expected = (
        (peers - 1)
        + jnp.where(plane > 0, 1, 0).astype(jnp.int32)
        + jnp.where(plane < planes - 1, 1, 0).astype(jnp.int32)
    )
    pl.semaphore_wait(barrier, expected)

    def cols(p, width):
        return pl.ds(pl.multiple_of(p * width, HEAD_WIDTH), width)

    def rows(p):
        return pl.ds(pl.multiple_of(p * tok, tok), tok)

    def in_pair(a, src_slot, dst_slot):
        if a == 0:
            return keys.at[:, cols(dst_slot, HEAD_WIDTH)], kv_all.at[plane, 0, rows(src_slot), :]
        if a == 1:
            return values.at[:, cols(dst_slot, HEAD_WIDTH)], kv_all.at[plane, 1, rows(src_slot), :]
        if a == 2:
            return query.at[:, cols(dst_slot, wide)], q_all.at[rows(src_slot), :]
        return grads.at[:, cols(dst_slot, wide)], g_all.at[rows(src_slot), :]

    def in_copy(a, src_slot, dst_slot):
        src, dst = in_pair(a, src_slot, dst_slot)
        return pltpu.make_async_remote_copy(
            src_ref=src, dst_ref=dst,
            send_sem=in_send.at[a, dst_slot], recv_sem=in_recv.at[a, src_slot],
            device_id=peer_id(dst_slot), device_id_type=MESH,
        )

    def own_copy(a):
        src, dst = in_pair(a, me, me)
        return pltpu.make_async_copy(src, dst, own_sem.at[a])

    def send_in(arrays):
        def one(d, _):
            for a in arrays:
                in_copy(a, me, (me + d) % peers).start()
            return 0

        lax.fori_loop(1, peers, one, 0)

    def await_in(arrays):
        for a in arrays:
            own_copy(a).wait()

        def one(d, _):
            for a in arrays:
                in_copy(a, (me + d) % peers, me).wait_recv()
            return 0

        lax.fori_loop(1, peers, one, 0)

    for a in range(4):
        own_copy(a).start()
    send_in((0, 1))

    def kv_copy(j, target):
        return pltpu.make_async_remote_copy(
            src_ref=kv_all.at[j], dst_ref=kv_all.at[j],
            send_sem=kv_send.at[j], recv_sem=kv_recv.at[j],
            device_id=plane_id(target), device_id_type=MESH,
        )

    await_in((0, 1))
    top_plane = plane == planes - 1

    @pl.when(plane < planes - 1)
    def _():
        kv_copy(plane, plane + 1).start()

    send_in((2,))

    def left(d, _):
        in_copy(2, me, (me + d) % peers).wait_send()
        return 0

    lax.fori_loop(1, peers, left, 0)
    send_in((3,))

    @pl.when(plane < planes - 1)
    def _():
        def relay(n, _):
            j = plane - 1 - n
            kv_copy(j, plane).wait_recv()
            kv_copy(j, plane + 1).start()
            return 0

        lax.fori_loop(0, plane, relay, 0)

    def spread(whole, by_rows, by_cols):
        for h in range(group):
            for s in range(splits):
                piece = whole[s * block:(s + 1) * block, h * HEAD_WIDTH:(h + 1) * HEAD_WIDTH]
                by_rows[(h * splits + s) * block:(h * splits + s + 1) * block] = piece
                by_cols[h * splits + s] = piece.T

    await_in((2,))
    spread(q_all, q_rows, q_cols)

    def masked(s, split):
        shape = s.shape
        key_pos = lax.broadcasted_iota(jnp.int32, shape, 0)
        query_pos = lax.broadcasted_iota(jnp.int32, shape, 1) + split * block
        return jnp.where(key_pos <= query_pos, s, MASKED)

    v_cols[...] = kv_all[plane, 1].T

    def first(h, _):
        for split in range(splits):
            i, seen = h * splits + split, (split + 1) * block
            s = masked(dot(kv_all[plane, 0, :seen], q_cols[i]), split)
            top = jnp.max(s, axis=0, keepdims=True)
            p = jnp.exp2((s - top) * LOG2_SCALE)
            row_max[i] = top
            row_sum[i] = jnp.sum(p, axis=0, keepdims=True)
            acc[i] = dot(v_cols[:, :seen], p.astype(jnp.bfloat16))
        return 0

    lax.fori_loop(0, group, first, 0, unroll=2)

    def take_grads():
        await_in((3,))
        spread(g_all, g_rows, g_cols)

    @pl.when(plane == 0)
    def _():
        take_grads()

    def forward(n, _):
        j = plane - 1 - n

        @pl.when(j == 0)
        def _():
            take_grads()

        @pl.when(top_plane)
        def _():
            kv_copy(j, plane).wait_recv()

        v_cols[...] = kv_all[j, 1].T

        def one(i, _):
            s = dot(kv_all[j, 0], q_cols[i])
            old = row_max[i]
            top = jnp.maximum(old, jnp.max(s, axis=0, keepdims=True))
            p = jnp.exp2((s - top) * LOG2_SCALE)
            shrink = jnp.exp2((old - top) * LOG2_SCALE)
            row_max[i] = top
            row_sum[i] = row_sum[i] * shrink + jnp.sum(p, axis=0, keepdims=True)
            acc[i] = acc[i] * shrink + dot(v_cols[...], p.astype(jnp.bfloat16))
            return 0

        lax.fori_loop(0, jobs, one, 0, unroll=4)
        return 0

    lax.fori_loop(0, plane, forward, 0)

    for i in range(jobs):
        total = row_sum[i]
        rounded = (acc[i] / total).astype(jnp.bfloat16)
        o_cols[i] = rounded
        lse[i] = row_max[i] * LOG2_SCALE + jnp.log2(total)
        delta[i] = jnp.sum(
            g_cols[i].astype(jnp.float32) * rounded.astype(jnp.float32), axis=0, keepdims=True
        )

    def out_pair(a, src_slot, dst_slot):
        if a == 0:
            return o_buf.at[rows(dst_slot), :], out_ref.at[:, cols(src_slot, wide)]
        if a == 1:
            return dq_buf.at[rows(dst_slot), :], dq_ref.at[:, cols(src_slot, wide)]
        if a == 2:
            return fin.at[0, rows(dst_slot), :], dk_ref.at[:, cols(src_slot, HEAD_WIDTH)]
        return fin.at[1, rows(dst_slot), :], dv_ref.at[:, cols(src_slot, HEAD_WIDTH)]

    def out_copy(a, src_slot, dst_slot):
        src, dst = out_pair(a, src_slot, dst_slot)
        return pltpu.make_async_remote_copy(
            src_ref=src, dst_ref=dst,
            send_sem=out_send.at[a, dst_slot], recv_sem=out_recv.at[a, src_slot],
            device_id=peer_id(dst_slot), device_id_type=MESH,
        )

    def own_out(a):
        src, dst = out_pair(a, me, me)
        return pltpu.make_async_copy(src, dst, own_sem.at[4 + a])

    def send_out(arrays):
        for a in arrays:
            own_out(a).start()

        def one(d, _):
            for a in arrays:
                out_copy(a, me, (me + d) % peers).start()
            return 0

        lax.fori_loop(1, peers, one, 0)

    dq_acc[...] = jnp.zeros_like(dq_acc)

    def part_copy(j, target):
        return pltpu.make_async_remote_copy(
            src_ref=part_out.at[j], dst_ref=part_in.at[j],
            send_sem=part_send.at[j], recv_sem=part_recv.at[j],
            device_id=plane_id(target), device_id_type=MESH,
        )

    def gradients(j, i, seen, split):
        where = pl.ds(i * block if isinstance(i, int) else pl.multiple_of(i * block, block), block)
        s = dot(kv_all[j, 0, :seen], q_cols[i])
        if split is not None:
            s = masked(s, split)
        p = jnp.exp2(s * LOG2_SCALE - lse[i])
        dp = dot(kv_all[j, 1, :seen], g_cols[i])
        ds = (p * (dp - delta[i])).astype(jnp.bfloat16)
        p_all[:seen, where] = p.astype(jnp.bfloat16)
        ds_all[:seen, where] = ds
        if seen < chunk:
            unseen = jnp.zeros((chunk - seen, block), jnp.bfloat16)
            p_all[seen:, where] = unseen
            ds_all[seen:, where] = unseen
        dq_acc[i] += dot(k_cols[:, :seen], ds)

    def backward(j, diagonal):
        k_cols[...] = kv_all[j, 0].T

        def one(i, _):
            gradients(j, i, chunk, None)
            return 0

        def triangle(h, _):
            for split in range(splits):
                gradients(j, h * splits + split, (split + 1) * block, split)
            return 0

        if diagonal:
            lax.fori_loop(0, group, triangle, 0, unroll=2)
        else:
            lax.fori_loop(0, jobs, one, 0, unroll=4)
        pair[j, 1] = dot(p_all[...], g_rows[...])
        pair[j, 0] = dot(ds_all[...], q_rows[...])

    def earlier(j, _):
        backward(j, False)

        @pl.when(top_plane)
        def _():
            part_out[j] = pair[j].astype(jnp.bfloat16)
            part_copy(j, plane - 1).start()

        return 0

    lax.fori_loop(0, plane, earlier, 0)

    def gather_cols(pieces, dst, factor):
        for h in range(group):
            for s in range(splits):
                piece = pieces[h * splits + s]
                if factor is not None:
                    piece = (piece * factor).astype(jnp.bfloat16)
                dst[s * block:(s + 1) * block, h * HEAD_WIDTH:(h + 1) * HEAD_WIDTH] = piece.T

    gather_cols(o_cols, o_buf, None)
    send_out((0,))
    backward(plane, True)
    gather_cols(dq_acc, dq_buf, SCALE)
    send_out((1,))

    @pl.when(plane < planes - 1)
    def _():
        def chain(j, _):
            part_copy(j, plane).wait_recv()
            part_out[j] = (pair[j] + part_in[j].astype(jnp.float32)).astype(jnp.bfloat16)
            part_copy(j, plane - 1).start()
            return 0

        lax.fori_loop(0, plane, chain, 0)
        part_copy(plane, plane).wait_recv()
        pair[plane] += part_in[plane].astype(jnp.float32)

    fin[0] = (pair[plane, 0] * SCALE).astype(jnp.bfloat16)
    fin[1] = pair[plane, 1].astype(jnp.bfloat16)
    send_out((2, 3))

    def drain(d, _):
        p = (me + d) % peers
        for a in (0, 1, 3):
            in_copy(a, me, p).wait_send()
        for a in range(4):
            out_copy(a, me, p).wait_send()
            out_copy(a, p, me).wait_recv()
        return 0

    lax.fori_loop(1, peers, drain, 0)
    for a in range(4):
        own_out(a).wait()

    @pl.when(plane < planes - 1)
    def _():
        def one(j, _):
            kv_copy(j, plane + 1).wait_send()
            return 0

        lax.fori_loop(0, plane + 1, one, 0)

    def sent(j, _):
        part_copy(j, plane - 1).wait_send()
        return 0

    lax.fori_loop(0, plane, sent, 0)


def hand_over(*refs):
    sources, results, held, sem = refs[:4], refs[4:8], refs[8:12], refs[12]
    loads = [pltpu.make_async_copy(sources[i], held[i], sem.at[0, i]) for i in range(4)]
    stores = [pltpu.make_async_copy(held[i], results[i], sem.at[1, i]) for i in range(4)]
    for load in loads:
        load.start()
    for load, store in zip(loads, stores):
        load.wait()
        store.start()
    for store in stores:
        store.wait()


def shards(query, keys, values, output_gradient):
    ctx = lax.axis_size("ctx")
    tp = lax.axis_size("tp")
    tok, model = query.shape
    kv_heads = keys.shape[1] // HEAD_WIDTH
    group = model // keys.shape[1]
    inner = kv_heads // tp
    planes = ctx // inner
    peers = kv_heads
    chunk = peers * tok
    block = min(256, chunk)
    jobs = group * (chunk // block)
    wide = group * HEAD_WIDTH
    bf16, f32 = jnp.bfloat16, jnp.float32
    anywhere = pl.BlockSpec(memory_space=pl.ANY)
    dma = pltpu.SemaphoreType.DMA
    results = pl.pallas_call(
        functools.partial(kernel, (tp, inner, planes, tok, group, block)),
        out_shape=tuple(
            jax.ShapeDtypeStruct(a.shape, a.dtype) for a in (query, query, keys, values)
        ),
        in_specs=[anywhere] * 4,
        out_specs=(anywhere,) * 4,
        scratch_shapes=[
            pltpu.VMEM((chunk, wide), bf16),
            pltpu.VMEM((chunk, wide), bf16),
            pltpu.VMEM((planes, 2, chunk, HEAD_WIDTH), bf16),
            pltpu.VMEM((chunk, wide), bf16),
            pltpu.VMEM((chunk, wide), bf16),
            pltpu.VMEM((2, chunk, HEAD_WIDTH), bf16),
            pltpu.VMEM((jobs * block, HEAD_WIDTH), bf16),
            pltpu.VMEM((jobs, HEAD_WIDTH, block), bf16),
            pltpu.VMEM((jobs * block, HEAD_WIDTH), bf16),
            pltpu.VMEM((jobs, HEAD_WIDTH, block), bf16),
            pltpu.VMEM((HEAD_WIDTH, chunk), bf16),
            pltpu.VMEM((HEAD_WIDTH, chunk), bf16),
            pltpu.VMEM((jobs, 1, block), f32),
            pltpu.VMEM((jobs, 1, block), f32),
            pltpu.VMEM((jobs, 1, block), f32),
            pltpu.VMEM((jobs, 1, block), f32),
            pltpu.VMEM((jobs, HEAD_WIDTH, block), f32),
            pltpu.VMEM((jobs, HEAD_WIDTH, block), bf16),
            pltpu.VMEM((jobs, HEAD_WIDTH, block), f32),
            pltpu.VMEM((chunk, jobs * block), bf16),
            pltpu.VMEM((chunk, jobs * block), bf16),
            pltpu.VMEM((planes, 2, chunk, HEAD_WIDTH), f32),
            pltpu.VMEM((planes, 2, chunk, HEAD_WIDTH), bf16),
            pltpu.VMEM((planes, 2, chunk, HEAD_WIDTH), bf16),
            dma((8,)),
            dma((4, peers)),
            dma((4, peers)),
            dma((planes,)),
            dma((planes,)),
            dma((planes,)),
            dma((planes,)),
            dma((4, peers)),
            dma((4, peers)),
        ],
        compiler_params=pltpu.CompilerParams(
            collective_id=0, has_side_effects=True, vmem_limit_bytes=64 * 1024 * 1024
        ),
    )(query, keys, values, output_gradient)
    return pl.pallas_call(
        hand_over,
        out_shape=tuple(jax.ShapeDtypeStruct(a.shape, a.dtype) for a in results),
        in_specs=[anywhere] * 4,
        out_specs=(anywhere,) * 4,
        scratch_shapes=[pltpu.VMEM(a.shape, a.dtype) for a in results] + [dma((2, 4))],
        compiler_params=pltpu.CompilerParams(vmem_limit_bytes=64 * 1024 * 1024),
    )(*results)


def solution(mesh):
    placed = (P(("ctx", "tp"), None),) * 4
    return jax.shard_map(
        shards, mesh=mesh, in_specs=placed, out_specs=placed, check_vma=False
    )
```

```python
import functools
import math

import jax
import jax.numpy as jnp
from jax import lax
from jax.experimental import pallas as pl
from jax.experimental.pallas import tpu as pltpu
from jax.sharding import PartitionSpec as P

HEAD_WIDTH = 128
MESH = pl.DeviceIdType.MESH
SCALE = HEAD_WIDTH ** (-0.5)
LOG2_SCALE = SCALE * math.log2(math.e)
MASKED = -1e30


def dot(a, b):
    return jnp.dot(a, b, preferred_element_type=jnp.float32)


def kernel(
    sizes,
    query, keys, values, grads,
    out_ref, dq_ref, dk_ref, dv_ref,
    q_all, g_all, kv_all, o_buf, dq_buf, fin,
    q_rows, q_cols, g_rows, g_cols, k_cols, v_cols,
    row_max, row_sum, lse, delta, acc, o_cols, dq_acc, p_all, ds_all, pair, part_out, part_in,
    own_sem, in_send, in_recv, kv_send, kv_recv, part_send, part_recv, out_send, out_recv, turn_sem,
):
    tp, inner, planes, tok, group, block = sizes
    peers = tp * inner
    chunk = peers * tok
    splits = chunk // block
    jobs = group * splits
    wide = group * HEAD_WIDTH
    ctx_index = lax.axis_index("ctx")
    tp_index = lax.axis_index("tp")
    plane = ctx_index // inner
    lane = ctx_index % inner
    me = lane * tp + tp_index

    def peer_id(p):
        return (plane * inner + p // tp, p % tp)

    def plane_id(z):
        return (z * inner + lane, tp_index)

    barrier = pltpu.get_barrier_semaphore()

    def greet(d, _):
        pl.semaphore_signal(
            barrier, inc=1, device_id=peer_id((me + d) % peers), device_id_type=MESH
        )
        return 0

    lax.fori_loop(1, peers, greet, 0)

    @pl.when(plane > 0)
    def _():
        pl.semaphore_signal(barrier, inc=1, device_id=plane_id(plane - 1), device_id_type=MESH)

    @pl.when(plane < planes - 1)
    def _():
        pl.semaphore_signal(barrier, inc=1, device_id=plane_id(plane + 1), device_id_type=MESH)

    expected = (
        (peers - 1)
        + jnp.where(plane > 0, 1, 0).astype(jnp.int32)
        + jnp.where(plane < planes - 1, 1, 0).astype(jnp.int32)
    )
    pl.semaphore_wait(barrier, expected)

    def cols(p, width):
        return pl.ds(pl.multiple_of(p * width, HEAD_WIDTH), width)

    def rows(p):
        return pl.ds(pl.multiple_of(p * tok, tok), tok)

    def in_pair(a, src_slot, dst_slot):
        if a == 0:
            return keys.at[:, cols(dst_slot, HEAD_WIDTH)], kv_all.at[plane, 0, rows(src_slot), :]
        if a == 1:
            return values.at[:, cols(dst_slot, HEAD_WIDTH)], kv_all.at[plane, 1, rows(src_slot), :]
        if a == 2:
            return query.at[:, cols(dst_slot, wide)], q_all.at[rows(src_slot), :]
        return grads.at[:, cols(dst_slot, wide)], g_all.at[rows(src_slot), :]

    def in_copy(a, src_slot, dst_slot):
        src, dst = in_pair(a, src_slot, dst_slot)
        return pltpu.make_async_remote_copy(
            src_ref=src, dst_ref=dst,
            send_sem=in_send.at[a, dst_slot], recv_sem=in_recv.at[a, src_slot],
            device_id=peer_id(dst_slot), device_id_type=MESH,
        )

    def own_copy(a):
        src, dst = in_pair(a, me, me)
        return pltpu.make_async_copy(src, dst, own_sem.at[a])

    def send_in(arrays):
        def one(d, _):
            for a in arrays:
                in_copy(a, me, (me + d) % peers).start()
            return 0

        lax.fori_loop(1, peers, one, 0)

    def await_in(arrays):
        for a in arrays:
            own_copy(a).wait()

        def one(d, _):
            for a in arrays:
                in_copy(a, (me + d) % peers, me).wait_recv()
            return 0

        lax.fori_loop(1, peers, one, 0)

    for a in range(4):
        own_copy(a).start()
    send_in((0, 1))

    def kv_copy(j, target):
        return pltpu.make_async_remote_copy(
            src_ref=kv_all.at[j], dst_ref=kv_all.at[j],
            send_sem=kv_send.at[j], recv_sem=kv_recv.at[j],
            device_id=plane_id(target), device_id_type=MESH,
        )

    await_in((0, 1))
    top_plane = plane == planes - 1

    staged = inner % 2 == 0
    leads = lane % 2 == 0 if staged else lane == lane
    below = plane < planes - 1

    def relay():
        def one(n, _):
            j = plane - 1 - n
            kv_copy(j, plane).wait_recv()
            kv_copy(j, plane + 1).start()
            return 0

        lax.fori_loop(0, plane, one, 0)

    @pl.when(below & leads)
    def _():
        kv_copy(plane, plane + 1).start()

    send_in((2,))

    @pl.when(top_plane)
    def _():
        def left(d, _):
            in_copy(2, me, (me + d) % peers).wait_send()
            return 0

        lax.fori_loop(1, peers, left, 0)

    send_in((3,))

    @pl.when(below & leads)
    def _():
        relay()

        def gone(j, _):
            kv_copy(j, plane + 1).wait_send()
            return 0

        lax.fori_loop(0, plane + 1, gone, 0)
        if staged:
            pl.semaphore_signal(
                turn_sem, inc=1, device_id=(ctx_index + 1, tp_index), device_id_type=MESH
            )

    if staged:
        @pl.when(below & (lane % 2 == 1))
        def _():
            pl.semaphore_wait(turn_sem, 1)
            kv_copy(plane, plane + 1).start()
            relay()

    def spread(whole, by_rows, by_cols):
        for h in range(group):
            for s in range(splits):
                piece = whole[s * block:(s + 1) * block, h * HEAD_WIDTH:(h + 1) * HEAD_WIDTH]
                by_rows[(h * splits + s) * block:(h * splits + s + 1) * block] = piece
                by_cols[h * splits + s] = piece.T

    await_in((2,))
    spread(q_all, q_rows, q_cols)

    def masked(s, split):
        shape = s.shape
        key_pos = lax.broadcasted_iota(jnp.int32, shape, 0)
        query_pos = lax.broadcasted_iota(jnp.int32, shape, 1) + split * block
        return jnp.where(key_pos <= query_pos, s, MASKED)

    v_cols[...] = kv_all[plane, 1].T

    def first(h, _):
        for split in range(splits):
            i, seen = h * splits + split, (split + 1) * block
            s = masked(dot(kv_all[plane, 0, :seen], q_cols[i]), split)
            top = jnp.max(s, axis=0, keepdims=True)
            p = jnp.exp2((s - top) * LOG2_SCALE)
            row_max[i] = top
            row_sum[i] = jnp.sum(p, axis=0, keepdims=True)
            acc[i] = dot(v_cols[:, :seen], p.astype(jnp.bfloat16))
        return 0

    lax.fori_loop(0, group, first, 0, unroll=2)

    def take_grads():
        await_in((3,))
        spread(g_all, g_rows, g_cols)

    @pl.when(plane == 0)
    def _():
        take_grads()

    def forward(n, _):
        j = plane - 1 - n

        @pl.when(j == 0)
        def _():
            take_grads()

        @pl.when(top_plane)
        def _():
            kv_copy(j, plane).wait_recv()

        v_cols[...] = kv_all[j, 1].T

        def one(i, _):
            s = dot(kv_all[j, 0], q_cols[i])
            old = row_max[i]
            top = jnp.maximum(old, jnp.max(s, axis=0, keepdims=True))
            p = jnp.exp2((s - top) * LOG2_SCALE)
            shrink = jnp.exp2((old - top) * LOG2_SCALE)
            row_max[i] = top
            row_sum[i] = row_sum[i] * shrink + jnp.sum(p, axis=0, keepdims=True)
            acc[i] = acc[i] * shrink + dot(v_cols[...], p.astype(jnp.bfloat16))
            return 0

        lax.fori_loop(0, jobs, one, 0, unroll=4)
        return 0

    lax.fori_loop(0, plane, forward, 0)

    for i in range(jobs):
        total = row_sum[i]
        rounded = (acc[i] / total).astype(jnp.bfloat16)
        o_cols[i] = rounded
        lse[i] = row_max[i] * LOG2_SCALE + jnp.log2(total)
        delta[i] = jnp.sum(
            g_cols[i].astype(jnp.float32) * rounded.astype(jnp.float32), axis=0, keepdims=True
        )

    def out_pair(a, src_slot, dst_slot):
        if a == 0:
            return o_buf.at[rows(dst_slot), :], out_ref.at[:, cols(src_slot, wide)]
        if a == 1:
            return dq_buf.at[rows(dst_slot), :], dq_ref.at[:, cols(src_slot, wide)]
        if a == 2:
            return fin.at[0, rows(dst_slot), :], dk_ref.at[:, cols(src_slot, HEAD_WIDTH)]
        return fin.at[1, rows(dst_slot), :], dv_ref.at[:, cols(src_slot, HEAD_WIDTH)]

    def out_copy(a, src_slot, dst_slot):
        src, dst = out_pair(a, src_slot, dst_slot)
        return pltpu.make_async_remote_copy(
            src_ref=src, dst_ref=dst,
            send_sem=out_send.at[a, dst_slot], recv_sem=out_recv.at[a, src_slot],
            device_id=peer_id(dst_slot), device_id_type=MESH,
        )

    def own_out(a):
        src, dst = out_pair(a, me, me)
        return pltpu.make_async_copy(src, dst, own_sem.at[4 + a])

    def send_out(arrays):
        for a in arrays:
            own_out(a).start()

        def one(d, _):
            for a in arrays:
                out_copy(a, me, (me + d) % peers).start()
            return 0

        lax.fori_loop(1, peers, one, 0)

    dq_acc[...] = jnp.zeros_like(dq_acc)

    def part_copy(j, target):
        return pltpu.make_async_remote_copy(
            src_ref=part_out.at[j], dst_ref=part_in.at[j],
            send_sem=part_send.at[j], recv_sem=part_recv.at[j],
            device_id=plane_id(target), device_id_type=MESH,
        )

    def gradients(j, i, seen, split):
        where = pl.ds(i * block if isinstance(i, int) else pl.multiple_of(i * block, block), block)
        s = dot(kv_all[j, 0, :seen], q_cols[i])
        if split is not None:
            s = masked(s, split)
        p = jnp.exp2(s * LOG2_SCALE - lse[i])
        dp = dot(kv_all[j, 1, :seen], g_cols[i])
        ds = (p * (dp - delta[i])).astype(jnp.bfloat16)
        p_all[:seen, where] = p.astype(jnp.bfloat16)
        ds_all[:seen, where] = ds
        if seen < chunk:
            unseen = jnp.zeros((chunk - seen, block), jnp.bfloat16)
            p_all[seen:, where] = unseen
            ds_all[seen:, where] = unseen
        dq_acc[i] += dot(k_cols[:, :seen], ds)

    def backward(j, diagonal):
        k_cols[...] = kv_all[j, 0].T

        def one(i, _):
            gradients(j, i, chunk, None)
            return 0

        def triangle(h, _):
            for split in range(splits):
                gradients(j, h * splits + split, (split + 1) * block, split)
            return 0

        if diagonal:
            lax.fori_loop(0, group, triangle, 0, unroll=2)
        else:
            lax.fori_loop(0, jobs, one, 0, unroll=4)
        pair[j, 1] = dot(p_all[...], g_rows[...])
        pair[j, 0] = dot(ds_all[...], q_rows[...])

    def earlier(j, _):
        backward(j, False)

        @pl.when(top_plane)
        def _():
            part_out[j] = pair[j].astype(jnp.bfloat16)
            part_copy(j, plane - 1).start()

        return 0

    lax.fori_loop(0, plane, earlier, 0)

    def gather_cols(pieces, dst, factor):
        for h in range(group):
            for s in range(splits):
                piece = pieces[h * splits + s]
                if factor is not None:
                    piece = (piece * factor).astype(jnp.bfloat16)
                dst[s * block:(s + 1) * block, h * HEAD_WIDTH:(h + 1) * HEAD_WIDTH] = piece.T

    gather_cols(o_cols, o_buf, None)
    send_out((0,))
    backward(plane, True)
    gather_cols(dq_acc, dq_buf, SCALE)
    send_out((1,))

    @pl.when(plane < planes - 1)
    def _():
        def chain(j, _):
            part_copy(j, plane).wait_recv()
            part_out[j] = (pair[j] + part_in[j].astype(jnp.float32)).astype(jnp.bfloat16)
            part_copy(j, plane - 1).start()
            return 0

        lax.fori_loop(0, plane, chain, 0)
        part_copy(plane, plane).wait_recv()
        pair[plane] += part_in[plane].astype(jnp.float32)

    fin[0] = (pair[plane, 0] * SCALE).astype(jnp.bfloat16)
    fin[1] = pair[plane, 1].astype(jnp.bfloat16)
    send_out((2, 3))

    def drain(d, _):
        p = (me + d) % peers
        for a in (0, 1, 3):
            in_copy(a, me, p).wait_send()

        @pl.when(below)
        def _():
            in_copy(2, me, p).wait_send()

        for a in range(4):
            out_copy(a, me, p).wait_send()
            out_copy(a, p, me).wait_recv()
        return 0

    lax.fori_loop(1, peers, drain, 0)
    for a in range(4):
        own_out(a).wait()

    if staged:
        @pl.when(below & (lane % 2 == 1))
        def _():
            def one(j, _):
                kv_copy(j, plane + 1).wait_send()
                return 0

            lax.fori_loop(0, plane + 1, one, 0)

    def sent(j, _):
        part_copy(j, plane - 1).wait_send()
        return 0

    lax.fori_loop(0, plane, sent, 0)


def hand_over(*refs):
    sources, results, held, sem = refs[:4], refs[4:8], refs[8:12], refs[12]
    loads = [pltpu.make_async_copy(sources[i], held[i], sem.at[0, i]) for i in range(4)]
    stores = [pltpu.make_async_copy(held[i], results[i], sem.at[1, i]) for i in range(4)]
    for load in loads:
        load.start()
    for load, store in zip(loads, stores):
        load.wait()
        store.start()
    for store in stores:
        store.wait()


def shards(query, keys, values, output_gradient):
    ctx = lax.axis_size("ctx")
    tp = lax.axis_size("tp")
    tok, model = query.shape
    kv_heads = keys.shape[1] // HEAD_WIDTH
    group = model // keys.shape[1]
    inner = kv_heads // tp
    planes = ctx // inner
    peers = kv_heads
    chunk = peers * tok
    block = min(256, chunk)
    jobs = group * (chunk // block)
    wide = group * HEAD_WIDTH
    bf16, f32 = jnp.bfloat16, jnp.float32
    anywhere = pl.BlockSpec(memory_space=pl.ANY)
    dma = pltpu.SemaphoreType.DMA
    results = pl.pallas_call(
        functools.partial(kernel, (tp, inner, planes, tok, group, block)),
        out_shape=tuple(
            jax.ShapeDtypeStruct(a.shape, a.dtype) for a in (query, query, keys, values)
        ),
        in_specs=[anywhere] * 4,
        out_specs=(anywhere,) * 4,
        scratch_shapes=[
            pltpu.VMEM((chunk, wide), bf16),
            pltpu.VMEM((chunk, wide), bf16),
            pltpu.VMEM((planes, 2, chunk, HEAD_WIDTH), bf16),
            pltpu.VMEM((chunk, wide), bf16),
            pltpu.VMEM((chunk, wide), bf16),
            pltpu.VMEM((2, chunk, HEAD_WIDTH), bf16),
            pltpu.VMEM((jobs * block, HEAD_WIDTH), bf16),
            pltpu.VMEM((jobs, HEAD_WIDTH, block), bf16),
            pltpu.VMEM((jobs * block, HEAD_WIDTH), bf16),
            pltpu.VMEM((jobs, HEAD_WIDTH, block), bf16),
            pltpu.VMEM((HEAD_WIDTH, chunk), bf16),
            pltpu.VMEM((HEAD_WIDTH, chunk), bf16),
            pltpu.VMEM((jobs, 1, block), f32),
            pltpu.VMEM((jobs, 1, block), f32),
            pltpu.VMEM((jobs, 1, block), f32),
            pltpu.VMEM((jobs, 1, block), f32),
            pltpu.VMEM((jobs, HEAD_WIDTH, block), f32),
            pltpu.VMEM((jobs, HEAD_WIDTH, block), bf16),
            pltpu.VMEM((jobs, HEAD_WIDTH, block), f32),
            pltpu.VMEM((chunk, jobs * block), bf16),
            pltpu.VMEM((chunk, jobs * block), bf16),
            pltpu.VMEM((planes, 2, chunk, HEAD_WIDTH), f32),
            pltpu.VMEM((planes, 2, chunk, HEAD_WIDTH), bf16),
            pltpu.VMEM((planes, 2, chunk, HEAD_WIDTH), bf16),
            dma((8,)),
            dma((4, peers)),
            dma((4, peers)),
            dma((planes,)),
            dma((planes,)),
            dma((planes,)),
            dma((planes,)),
            dma((4, peers)),
            dma((4, peers)),
            pltpu.SemaphoreType.REGULAR,
        ],
        compiler_params=pltpu.CompilerParams(
            collective_id=0, has_side_effects=True, vmem_limit_bytes=64 * 1024 * 1024
        ),
    )(query, keys, values, output_gradient)
    return pl.pallas_call(
        hand_over,
        out_shape=tuple(jax.ShapeDtypeStruct(a.shape, a.dtype) for a in results),
        in_specs=[anywhere] * 4,
        out_specs=(anywhere,) * 4,
        scratch_shapes=[pltpu.VMEM(a.shape, a.dtype) for a in results] + [dma((2, 4))],
        compiler_params=pltpu.CompilerParams(vmem_limit_bytes=64 * 1024 * 1024),
    )(*results)


def solution(mesh):
    placed = (P(("ctx", "tp"), None),) * 4
    return jax.shard_map(
        shards, mesh=mesh, in_specs=placed, out_specs=placed, check_vma=False
    )
```

```python
import functools
import math

import jax
import jax.numpy as jnp
from jax import lax
from jax.experimental import pallas as pl
from jax.experimental.pallas import tpu as pltpu
from jax.sharding import PartitionSpec as P

HEAD_WIDTH = 128
MESH = pl.DeviceIdType.MESH
SCALE = HEAD_WIDTH ** (-0.5)
LOG2_SCALE = SCALE * math.log2(math.e)
MASKED = -1e30


def dot(a, b):
    return jnp.dot(a, b, preferred_element_type=jnp.float32)


def kernel(
    sizes,
    query_hbm, keys_hbm, values_hbm, grads_hbm,
    out_hbm, dq_hbm, dk_hbm, dv_hbm,
    query, keys, values, grads,
    out_ref, dq_ref, dk_ref, dv_ref,
    q_all, g_all, kv_all, o_buf, dq_buf, fin,
    q_rows, q_cols, g_rows, g_cols, k_cols, v_cols,
    row_max, row_sum, lse, delta, acc, o_cols, dq_acc, p_all, ds_all, pair, part_out, part_in,
    own_sem, in_send, in_recv, kv_send, kv_recv, part_send, part_recv, out_send, out_recv, load_sem, turn_sem,
):
    tp, inner, planes, tok, group, block = sizes
    peers = tp * inner
    chunk = peers * tok
    splits = chunk // block
    jobs = group * splits
    wide = group * HEAD_WIDTH
    ctx_index = lax.axis_index("ctx")
    tp_index = lax.axis_index("tp")
    plane = ctx_index // inner
    lane = ctx_index % inner
    me = lane * tp + tp_index

    def peer_id(p):
        return (plane * inner + p // tp, p % tp)

    def plane_id(z):
        return (z * inner + lane, tp_index)

    loads = [
        pltpu.make_async_copy(src, dst, load_sem.at[n])
        for n, (src, dst) in enumerate(
            ((keys_hbm, keys), (values_hbm, values), (query_hbm, query), (grads_hbm, grads))
        )
    ]
    for load in loads:
        load.start()

    barrier = pltpu.get_barrier_semaphore()

    def greet(d, _):
        pl.semaphore_signal(
            barrier, inc=1, device_id=peer_id((me + d) % peers), device_id_type=MESH
        )
        return 0

    lax.fori_loop(1, peers, greet, 0)

    @pl.when(plane > 0)
    def _():
        pl.semaphore_signal(barrier, inc=1, device_id=plane_id(plane - 1), device_id_type=MESH)

    @pl.when(plane < planes - 1)
    def _():
        pl.semaphore_signal(barrier, inc=1, device_id=plane_id(plane + 1), device_id_type=MESH)

    expected = (
        (peers - 1)
        + jnp.where(plane > 0, 1, 0).astype(jnp.int32)
        + jnp.where(plane < planes - 1, 1, 0).astype(jnp.int32)
    )
    pl.semaphore_wait(barrier, expected)

    def cols(p, width):
        return pl.ds(pl.multiple_of(p * width, HEAD_WIDTH), width)

    def rows(p):
        return pl.ds(pl.multiple_of(p * tok, tok), tok)

    def in_pair(a, src_slot, dst_slot):
        if a == 0:
            return keys.at[:, cols(dst_slot, HEAD_WIDTH)], kv_all.at[plane, 0, rows(src_slot), :]
        if a == 1:
            return values.at[:, cols(dst_slot, HEAD_WIDTH)], kv_all.at[plane, 1, rows(src_slot), :]
        if a == 2:
            return query.at[:, cols(dst_slot, wide)], q_all.at[rows(src_slot), :]
        return grads.at[:, cols(dst_slot, wide)], g_all.at[rows(src_slot), :]

    def in_copy(a, src_slot, dst_slot):
        src, dst = in_pair(a, src_slot, dst_slot)
        return pltpu.make_async_remote_copy(
            src_ref=src, dst_ref=dst,
            send_sem=in_send.at[a, dst_slot], recv_sem=in_recv.at[a, src_slot],
            device_id=peer_id(dst_slot), device_id_type=MESH,
        )

    def own_copy(a):
        src, dst = in_pair(a, me, me)
        return pltpu.make_async_copy(src, dst, own_sem.at[a])

    def send_in(arrays):
        def one(d, _):
            for a in arrays:
                in_copy(a, me, (me + d) % peers).start()
            return 0

        lax.fori_loop(1, peers, one, 0)

    def await_in(arrays):
        for a in arrays:
            own_copy(a).wait()

        def one(d, _):
            for a in arrays:
                in_copy(a, (me + d) % peers, me).wait_recv()
            return 0

        lax.fori_loop(1, peers, one, 0)

    for load in loads:
        load.wait()
    for a in range(4):
        own_copy(a).start()
    send_in((0, 1))

    def kv_copy(j, target):
        return pltpu.make_async_remote_copy(
            src_ref=kv_all.at[j], dst_ref=kv_all.at[j],
            send_sem=kv_send.at[j], recv_sem=kv_recv.at[j],
            device_id=plane_id(target), device_id_type=MESH,
        )

    await_in((0, 1))
    top_plane = plane == planes - 1

    staged = inner % 2 == 0
    leads = lane % 2 == 0 if staged else lane == lane
    below = plane < planes - 1

    def relay():
        def one(n, _):
            j = plane - 1 - n
            kv_copy(j, plane).wait_recv()
            kv_copy(j, plane + 1).start()
            return 0

        lax.fori_loop(0, plane, one, 0)

    @pl.when(below & leads)
    def _():
        kv_copy(plane, plane + 1).start()

    send_in((2,))

    @pl.when(top_plane)
    def _():
        def left(d, _):
            in_copy(2, me, (me + d) % peers).wait_send()
            return 0

        lax.fori_loop(1, peers, left, 0)

    send_in((3,))

    @pl.when(below & leads)
    def _():
        relay()

        def gone(j, _):
            kv_copy(j, plane + 1).wait_send()
            return 0

        lax.fori_loop(0, plane + 1, gone, 0)
        if staged:
            pl.semaphore_signal(
                turn_sem, inc=1, device_id=(ctx_index + 1, tp_index), device_id_type=MESH
            )

    if staged:
        @pl.when(below & (lane % 2 == 1))
        def _():
            pl.semaphore_wait(turn_sem, 1)
            kv_copy(plane, plane + 1).start()
            relay()

    def spread(whole, by_rows, by_cols):
        for h in range(group):
            for s in range(splits):
                piece = whole[s * block:(s + 1) * block, h * HEAD_WIDTH:(h + 1) * HEAD_WIDTH]
                by_rows[(h * splits + s) * block:(h * splits + s + 1) * block] = piece
                by_cols[h * splits + s] = piece.T

    await_in((2,))
    spread(q_all, q_rows, q_cols)

    def masked(s, split):
        shape = s.shape
        key_pos = lax.broadcasted_iota(jnp.int32, shape, 0)
        query_pos = lax.broadcasted_iota(jnp.int32, shape, 1) + split * block
        return jnp.where(key_pos <= query_pos, s, MASKED)

    v_cols[...] = kv_all[plane, 1].T

    def first(h, _):
        for split in range(splits):
            i, seen = h * splits + split, (split + 1) * block
            s = masked(dot(kv_all[plane, 0, :seen], q_cols[i]), split)
            top = jnp.max(s, axis=0, keepdims=True)
            p = jnp.exp2((s - top) * LOG2_SCALE)
            row_max[i] = top
            row_sum[i] = jnp.sum(p, axis=0, keepdims=True)
            acc[i] = dot(v_cols[:, :seen], p.astype(jnp.bfloat16))
        return 0

    lax.fori_loop(0, group, first, 0, unroll=2)

    def take_grads():
        await_in((3,))
        spread(g_all, g_rows, g_cols)

    @pl.when(plane == 0)
    def _():
        take_grads()

    def forward(n, _):
        j = plane - 1 - n

        @pl.when(j == 0)
        def _():
            take_grads()

        @pl.when(top_plane)
        def _():
            kv_copy(j, plane).wait_recv()

        v_cols[...] = kv_all[j, 1].T

        def one(i, _):
            s = dot(kv_all[j, 0], q_cols[i])
            old = row_max[i]
            top = jnp.maximum(old, jnp.max(s, axis=0, keepdims=True))
            p = jnp.exp2((s - top) * LOG2_SCALE)
            shrink = jnp.exp2((old - top) * LOG2_SCALE)
            row_max[i] = top
            row_sum[i] = row_sum[i] * shrink + jnp.sum(p, axis=0, keepdims=True)
            acc[i] = acc[i] * shrink + dot(v_cols[...], p.astype(jnp.bfloat16))
            return 0

        lax.fori_loop(0, jobs, one, 0, unroll=4)
        return 0

    lax.fori_loop(0, plane, forward, 0)

    for i in range(jobs):
        total = row_sum[i]
        rounded = (acc[i] / total).astype(jnp.bfloat16)
        o_cols[i] = rounded
        lse[i] = row_max[i] * LOG2_SCALE + jnp.log2(total)
        delta[i] = jnp.sum(
            g_cols[i].astype(jnp.float32) * rounded.astype(jnp.float32), axis=0, keepdims=True
        )

    def out_pair(a, src_slot, dst_slot):
        if a == 0:
            return o_buf.at[rows(dst_slot), :], out_ref.at[:, cols(src_slot, wide)]
        if a == 1:
            return dq_buf.at[rows(dst_slot), :], dq_ref.at[:, cols(src_slot, wide)]
        if a == 2:
            return fin.at[0, rows(dst_slot), :], dk_ref.at[:, cols(src_slot, HEAD_WIDTH)]
        return fin.at[1, rows(dst_slot), :], dv_ref.at[:, cols(src_slot, HEAD_WIDTH)]

    def out_copy(a, src_slot, dst_slot):
        src, dst = out_pair(a, src_slot, dst_slot)
        return pltpu.make_async_remote_copy(
            src_ref=src, dst_ref=dst,
            send_sem=out_send.at[a, dst_slot], recv_sem=out_recv.at[a, src_slot],
            device_id=peer_id(dst_slot), device_id_type=MESH,
        )

    def own_out(a):
        src, dst = out_pair(a, me, me)
        return pltpu.make_async_copy(src, dst, own_sem.at[4 + a])

    def send_out(arrays):
        for a in arrays:
            own_out(a).start()

        def one(d, _):
            for a in arrays:
                out_copy(a, me, (me + d) % peers).start()
            return 0

        lax.fori_loop(1, peers, one, 0)

    dq_acc[...] = jnp.zeros_like(dq_acc)

    def part_copy(j, target):
        return pltpu.make_async_remote_copy(
            src_ref=part_out.at[j], dst_ref=part_in.at[j],
            send_sem=part_send.at[j], recv_sem=part_recv.at[j],
            device_id=plane_id(target), device_id_type=MESH,
        )

    def gradients(j, i, seen, split):
        where = pl.ds(i * block if isinstance(i, int) else pl.multiple_of(i * block, block), block)
        s = dot(kv_all[j, 0, :seen], q_cols[i])
        if split is not None:
            s = masked(s, split)
        p = jnp.exp2(s * LOG2_SCALE - lse[i])
        dp = dot(kv_all[j, 1, :seen], g_cols[i])
        ds = (p * (dp - delta[i])).astype(jnp.bfloat16)
        p_all[:seen, where] = p.astype(jnp.bfloat16)
        ds_all[:seen, where] = ds
        if seen < chunk:
            unseen = jnp.zeros((chunk - seen, block), jnp.bfloat16)
            p_all[seen:, where] = unseen
            ds_all[seen:, where] = unseen
        dq_acc[i] += dot(k_cols[:, :seen], ds)

    def backward(j, diagonal):
        k_cols[...] = kv_all[j, 0].T

        def one(i, _):
            gradients(j, i, chunk, None)
            return 0

        def triangle(h, _):
            for split in range(splits):
                gradients(j, h * splits + split, (split + 1) * block, split)
            return 0

        if diagonal:
            lax.fori_loop(0, group, triangle, 0, unroll=2)
        else:
            lax.fori_loop(0, jobs, one, 0, unroll=4)
        pair[j, 1] = dot(p_all[...], g_rows[...])
        pair[j, 0] = dot(ds_all[...], q_rows[...])

    def earlier(j, _):
        backward(j, False)

        @pl.when(top_plane)
        def _():
            part_out[j] = pair[j].astype(jnp.bfloat16)
            part_copy(j, plane - 1).start()

        return 0

    lax.fori_loop(0, plane, earlier, 0)

    def gather_cols(pieces, dst, factor):
        for h in range(group):
            for s in range(splits):
                piece = pieces[h * splits + s]
                if factor is not None:
                    piece = (piece * factor).astype(jnp.bfloat16)
                dst[s * block:(s + 1) * block, h * HEAD_WIDTH:(h + 1) * HEAD_WIDTH] = piece.T

    gather_cols(o_cols, o_buf, None)
    send_out((0,))
    backward(plane, True)
    gather_cols(dq_acc, dq_buf, SCALE)
    send_out((1,))

    @pl.when(plane < planes - 1)
    def _():
        def chain(j, _):
            part_copy(j, plane).wait_recv()
            part_out[j] = (pair[j] + part_in[j].astype(jnp.float32)).astype(jnp.bfloat16)
            part_copy(j, plane - 1).start()
            return 0

        lax.fori_loop(0, plane, chain, 0)
        part_copy(plane, plane).wait_recv()
        pair[plane] += part_in[plane].astype(jnp.float32)

    fin[0] = (pair[plane, 0] * SCALE).astype(jnp.bfloat16)
    fin[1] = pair[plane, 1].astype(jnp.bfloat16)
    send_out((2, 3))

    def drain(d, _):
        p = (me + d) % peers
        for a in (0, 1, 3):
            in_copy(a, me, p).wait_send()

        @pl.when(below)
        def _():
            in_copy(2, me, p).wait_send()

        for a in range(4):
            out_copy(a, me, p).wait_send()
            out_copy(a, p, me).wait_recv()
        return 0

    lax.fori_loop(1, peers, drain, 0)
    for a in range(4):
        own_out(a).wait()
    stores = [
        pltpu.make_async_copy(src, dst, load_sem.at[4 + n])
        for n, (src, dst) in enumerate(
            ((out_ref, out_hbm), (dq_ref, dq_hbm), (dk_ref, dk_hbm), (dv_ref, dv_hbm))
        )
    ]
    for store in stores:
        store.start()

    if staged:
        @pl.when(below & (lane % 2 == 1))
        def _():
            def one(j, _):
                kv_copy(j, plane + 1).wait_send()
                return 0

            lax.fori_loop(0, plane + 1, one, 0)

    def sent(j, _):
        part_copy(j, plane - 1).wait_send()
        return 0

    lax.fori_loop(0, plane, sent, 0)
    for store in stores:
        store.wait()


def hand_over(*refs):
    sources, results, held, sem = refs[:4], refs[4:8], refs[8:12], refs[12]
    loads = [pltpu.make_async_copy(sources[i], held[i], sem.at[0, i]) for i in range(4)]
    stores = [pltpu.make_async_copy(held[i], results[i], sem.at[1, i]) for i in range(4)]
    for load in loads:
        load.start()
    for load, store in zip(loads, stores):
        load.wait()
        store.start()
    for store in stores:
        store.wait()


def shards(query, keys, values, output_gradient):
    ctx = lax.axis_size("ctx")
    tp = lax.axis_size("tp")
    tok, model = query.shape
    kv_heads = keys.shape[1] // HEAD_WIDTH
    group = model // keys.shape[1]
    inner = kv_heads // tp
    planes = ctx // inner
    peers = kv_heads
    chunk = peers * tok
    block = min(256, chunk)
    jobs = group * (chunk // block)
    wide = group * HEAD_WIDTH
    bf16, f32 = jnp.bfloat16, jnp.float32
    anywhere = pl.BlockSpec(memory_space=pl.ANY)
    dma = pltpu.SemaphoreType.DMA
    results = pl.pallas_call(
        functools.partial(kernel, (tp, inner, planes, tok, group, block)),
        out_shape=tuple(
            jax.ShapeDtypeStruct(a.shape, a.dtype) for a in (query, query, keys, values)
        ),
        in_specs=[anywhere] * 4,
        out_specs=(anywhere,) * 4,
        scratch_shapes=[
            pltpu.VMEM(a.shape, a.dtype)
            for a in (query, keys, values, output_gradient, query, query, keys, values)
        ] + [
            pltpu.VMEM((chunk, wide), bf16),
            pltpu.VMEM((chunk, wide), bf16),
            pltpu.VMEM((planes, 2, chunk, HEAD_WIDTH), bf16),
            pltpu.VMEM((chunk, wide), bf16),
            pltpu.VMEM((chunk, wide), bf16),
            pltpu.VMEM((2, chunk, HEAD_WIDTH), bf16),
            pltpu.VMEM((jobs * block, HEAD_WIDTH), bf16),
            pltpu.VMEM((jobs, HEAD_WIDTH, block), bf16),
            pltpu.VMEM((jobs * block, HEAD_WIDTH), bf16),
            pltpu.VMEM((jobs, HEAD_WIDTH, block), bf16),
            pltpu.VMEM((HEAD_WIDTH, chunk), bf16),
            pltpu.VMEM((HEAD_WIDTH, chunk), bf16),
            pltpu.VMEM((jobs, 1, block), f32),
            pltpu.VMEM((jobs, 1, block), f32),
            pltpu.VMEM((jobs, 1, block), f32),
            pltpu.VMEM((jobs, 1, block), f32),
            pltpu.VMEM((jobs, HEAD_WIDTH, block), f32),
            pltpu.VMEM((jobs, HEAD_WIDTH, block), bf16),
            pltpu.VMEM((jobs, HEAD_WIDTH, block), f32),
            pltpu.VMEM((chunk, jobs * block), bf16),
            pltpu.VMEM((chunk, jobs * block), bf16),
            pltpu.VMEM((planes, 2, chunk, HEAD_WIDTH), f32),
            pltpu.VMEM((planes, 2, chunk, HEAD_WIDTH), bf16),
            pltpu.VMEM((planes, 2, chunk, HEAD_WIDTH), bf16),
            dma((8,)),
            dma((4, peers)),
            dma((4, peers)),
            dma((planes,)),
            dma((planes,)),
            dma((planes,)),
            dma((planes,)),
            dma((4, peers)),
            dma((4, peers)),
            dma((8,)),
            pltpu.SemaphoreType.REGULAR,
        ],
        compiler_params=pltpu.CompilerParams(
            collective_id=0, has_side_effects=True, vmem_limit_bytes=64 * 1024 * 1024
        ),
    )(query, keys, values, output_gradient)
    return pl.pallas_call(
        hand_over,
        out_shape=tuple(jax.ShapeDtypeStruct(a.shape, a.dtype) for a in results),
        in_specs=[anywhere] * 4,
        out_specs=(anywhere,) * 4,
        scratch_shapes=[pltpu.VMEM(a.shape, a.dtype) for a in results] + [dma((2, 4))],
        compiler_params=pltpu.CompilerParams(vmem_limit_bytes=64 * 1024 * 1024),
    )(*results)


def solution(mesh):
    placed = (P(("ctx", "tp"), None),) * 4
    return jax.shard_map(
        shards, mesh=mesh, in_specs=placed, out_specs=placed, check_vma=False
    )
```

```python
import functools
import math

import jax
import jax.numpy as jnp
from jax import lax
from jax.experimental import pallas as pl
from jax.experimental.pallas import tpu as pltpu
from jax.sharding import PartitionSpec as P

HEAD_WIDTH = 128
MESH = pl.DeviceIdType.MESH
SCALE = HEAD_WIDTH ** (-0.5)
LOG2_SCALE = SCALE * math.log2(math.e)
MASKED = -1e30


def dot(a, b):
    return jnp.dot(a, b, preferred_element_type=jnp.float32)


def kernel(
    sizes,
    query, keys, values, grads,
    out_ref, dq_ref, dk_ref, dv_ref,
    q_all, g_all, kv_all, o_buf, dq_buf, fin,
    q_rows, q_cols, g_rows, g_cols, k_cols, v_cols,
    row_max, row_sum, lse, delta, acc, o_cols, dq_acc, p_all, ds_all, s_all, dp_all, pair, part_out, part_in,
    own_sem, in_send, in_recv, kv_send, kv_recv, part_send, part_recv, out_send, out_recv, turn_sem,
):
    tp, inner, planes, tok, group, block = sizes
    peers = tp * inner
    chunk = peers * tok
    splits = chunk // block
    jobs = group * splits
    wide = group * HEAD_WIDTH
    ctx_index = lax.axis_index("ctx")
    tp_index = lax.axis_index("tp")
    plane = ctx_index // inner
    lane = ctx_index % inner
    me = lane * tp + tp_index

    def peer_id(p):
        return (plane * inner + p // tp, p % tp)

    def plane_id(z):
        return (z * inner + lane, tp_index)

    barrier = pltpu.get_barrier_semaphore()

    def greet(d, _):
        pl.semaphore_signal(
            barrier, inc=1, device_id=peer_id((me + d) % peers), device_id_type=MESH
        )
        return 0

    lax.fori_loop(1, peers, greet, 0)

    @pl.when(plane > 0)
    def _():
        pl.semaphore_signal(barrier, inc=1, device_id=plane_id(plane - 1), device_id_type=MESH)

    @pl.when(plane < planes - 1)
    def _():
        pl.semaphore_signal(barrier, inc=1, device_id=plane_id(plane + 1), device_id_type=MESH)

    expected = (
        (peers - 1)
        + jnp.where(plane > 0, 1, 0).astype(jnp.int32)
        + jnp.where(plane < planes - 1, 1, 0).astype(jnp.int32)
    )
    pl.semaphore_wait(barrier, expected)

    def cols(p, width):
        return pl.ds(pl.multiple_of(p * width, HEAD_WIDTH), width)

    def rows(p):
        return pl.ds(pl.multiple_of(p * tok, tok), tok)

    def in_pair(a, src_slot, dst_slot):
        if a == 0:
            return keys.at[:, cols(dst_slot, HEAD_WIDTH)], kv_all.at[plane, 0, rows(src_slot), :]
        if a == 1:
            return values.at[:, cols(dst_slot, HEAD_WIDTH)], kv_all.at[plane, 1, rows(src_slot), :]
        if a == 2:
            return query.at[:, cols(dst_slot, wide)], q_all.at[rows(src_slot), :]
        return grads.at[:, cols(dst_slot, wide)], g_all.at[rows(src_slot), :]

    def in_copy(a, src_slot, dst_slot):
        src, dst = in_pair(a, src_slot, dst_slot)
        return pltpu.make_async_remote_copy(
            src_ref=src, dst_ref=dst,
            send_sem=in_send.at[a, dst_slot], recv_sem=in_recv.at[a, src_slot],
            device_id=peer_id(dst_slot), device_id_type=MESH,
        )

    def own_copy(a):
        src, dst = in_pair(a, me, me)
        return pltpu.make_async_copy(src, dst, own_sem.at[a])

    def send_in(arrays):
        def one(d, _):
            for a in arrays:
                in_copy(a, me, (me + d) % peers).start()
            return 0

        lax.fori_loop(1, peers, one, 0)

    def await_in(arrays):
        for a in arrays:
            own_copy(a).wait()

        def one(d, _):
            for a in arrays:
                in_copy(a, (me + d) % peers, me).wait_recv()
            return 0

        lax.fori_loop(1, peers, one, 0)

    for a in range(4):
        own_copy(a).start()
    send_in((0, 1))

    def kv_copy(j, target):
        return pltpu.make_async_remote_copy(
            src_ref=kv_all.at[j], dst_ref=kv_all.at[j],
            send_sem=kv_send.at[j], recv_sem=kv_recv.at[j],
            device_id=plane_id(target), device_id_type=MESH,
        )

    await_in((0, 1))
    top_plane = plane == planes - 1

    staged = inner % 2 == 0
    leads = lane % 2 == 0 if staged else lane == lane
    below = plane < planes - 1

    def relay():
        def one(n, _):
            j = plane - 1 - n
            kv_copy(j, plane).wait_recv()
            kv_copy(j, plane + 1).start()
            return 0

        lax.fori_loop(0, plane, one, 0)

    @pl.when(below & leads)
    def _():
        kv_copy(plane, plane + 1).start()

    send_in((2,))

    @pl.when(top_plane)
    def _():
        def left(d, _):
            in_copy(2, me, (me + d) % peers).wait_send()
            return 0

        lax.fori_loop(1, peers, left, 0)

    send_in((3,))

    @pl.when(below & leads)
    def _():
        relay()

        def gone(j, _):
            kv_copy(j, plane + 1).wait_send()
            return 0

        lax.fori_loop(0, plane + 1, gone, 0)
        if staged:
            pl.semaphore_signal(
                turn_sem, inc=1, device_id=(ctx_index + 1, tp_index), device_id_type=MESH
            )

    if staged:
        @pl.when(below & (lane % 2 == 1))
        def _():
            pl.semaphore_wait(turn_sem, 1)
            kv_copy(plane, plane + 1).start()
            relay()

    def spread(whole, by_rows, by_cols):
        for h in range(group):
            for s in range(splits):
                piece = whole[s * block:(s + 1) * block, h * HEAD_WIDTH:(h + 1) * HEAD_WIDTH]
                by_rows[(h * splits + s) * block:(h * splits + s + 1) * block] = piece
                by_cols[h * splits + s] = piece.T

    await_in((2,))
    spread(q_all, q_rows, q_cols)

    def masked(s, split):
        shape = s.shape
        key_pos = lax.broadcasted_iota(jnp.int32, shape, 0)
        query_pos = lax.broadcasted_iota(jnp.int32, shape, 1) + split * block
        return jnp.where(key_pos <= query_pos, s, MASKED)

    v_cols[...] = kv_all[plane, 1].T

    def first(h, _):
        for split in range(splits):
            i, seen = h * splits + split, (split + 1) * block
            s = masked(dot(kv_all[plane, 0, :seen], q_cols[i]) * LOG2_SCALE, split)
            top = jnp.max(s, axis=0, keepdims=True)
            p = jnp.exp2(s - top)
            row_max[i] = top
            row_sum[i] = jnp.sum(p, axis=0, keepdims=True)
            acc[i] = dot(v_cols[:, :seen], p.astype(jnp.bfloat16))
        return 0

    lax.fori_loop(0, group, first, 0, unroll=2)

    await_in((3,))
    spread(g_all, g_rows, g_cols)

    def forward(n, _):
        j = plane - 1 - n

        @pl.when(top_plane)
        def _():
            kv_copy(j, plane).wait_recv()

        v_cols[...] = kv_all[j, 1].T

        def one(i, _):
            s = dot(kv_all[j, 0], q_cols[i]) * LOG2_SCALE
            s_all[j, i] = s
            dp_all[j, i] = dot(kv_all[j, 1], g_cols[i])
            old = row_max[i]
            top = jnp.maximum(old, jnp.max(s, axis=0, keepdims=True))
            p = jnp.exp2(s - top)
            shrink = jnp.exp2(old - top)
            row_max[i] = top
            row_sum[i] = row_sum[i] * shrink + jnp.sum(p, axis=0, keepdims=True)
            acc[i] = acc[i] * shrink + dot(v_cols[...], p.astype(jnp.bfloat16))
            return 0

        lax.fori_loop(0, jobs, one, 0, unroll=4)
        return 0

    lax.fori_loop(0, plane, forward, 0)

    for i in range(jobs):
        total = row_sum[i]
        rounded = (acc[i] / total).astype(jnp.bfloat16)
        o_cols[i] = rounded
        lse[i] = row_max[i] + jnp.log2(total)
        delta[i] = jnp.sum(
            g_cols[i].astype(jnp.float32) * rounded.astype(jnp.float32), axis=0, keepdims=True
        )

    def out_pair(a, src_slot, dst_slot):
        if a == 0:
            return o_buf.at[rows(dst_slot), :], out_ref.at[:, cols(src_slot, wide)]
        if a == 1:
            return dq_buf.at[rows(dst_slot), :], dq_ref.at[:, cols(src_slot, wide)]
        if a == 2:
            return fin.at[0, rows(dst_slot), :], dk_ref.at[:, cols(src_slot, HEAD_WIDTH)]
        return fin.at[1, rows(dst_slot), :], dv_ref.at[:, cols(src_slot, HEAD_WIDTH)]

    def out_copy(a, src_slot, dst_slot):
        src, dst = out_pair(a, src_slot, dst_slot)
        return pltpu.make_async_remote_copy(
            src_ref=src, dst_ref=dst,
            send_sem=out_send.at[a, dst_slot], recv_sem=out_recv.at[a, src_slot],
            device_id=peer_id(dst_slot), device_id_type=MESH,
        )

    def own_out(a):
        src, dst = out_pair(a, me, me)
        return pltpu.make_async_copy(src, dst, own_sem.at[4 + a])

    def send_out(arrays):
        for a in arrays:
            own_out(a).start()

        def one(d, _):
            for a in arrays:
                out_copy(a, me, (me + d) % peers).start()
            return 0

        lax.fori_loop(1, peers, one, 0)

    dq_acc[...] = jnp.zeros_like(dq_acc)

    def part_copy(j, target):
        return pltpu.make_async_remote_copy(
            src_ref=part_out.at[j], dst_ref=part_in.at[j],
            send_sem=part_send.at[j], recv_sem=part_recv.at[j],
            device_id=plane_id(target), device_id_type=MESH,
        )

    def gradients(j, i, seen, split):
        where = pl.ds(i * block if isinstance(i, int) else pl.multiple_of(i * block, block), block)
        if split is not None:
            s = masked(dot(kv_all[j, 0, :seen], q_cols[i]) * LOG2_SCALE, split)
            dp = dot(kv_all[j, 1, :seen], g_cols[i])
        else:
            s, dp = s_all[j, i], dp_all[j, i]
        p = jnp.exp2(s - lse[i])
        ds = (p * (dp - delta[i])).astype(jnp.bfloat16)
        p_all[:seen, where] = p.astype(jnp.bfloat16)
        ds_all[:seen, where] = ds
        if seen < chunk:
            unseen = jnp.zeros((chunk - seen, block), jnp.bfloat16)
            p_all[seen:, where] = unseen
            ds_all[seen:, where] = unseen
        dq_acc[i] += dot(k_cols[:, :seen], ds)

    def backward(j, diagonal):
        k_cols[...] = kv_all[j, 0].T

        def one(i, _):
            gradients(j, i, chunk, None)
            return 0

        def triangle(h, _):
            for split in range(splits):
                gradients(j, h * splits + split, (split + 1) * block, split)
            return 0

        if diagonal:
            lax.fori_loop(0, group, triangle, 0, unroll=2)
        else:
            lax.fori_loop(0, jobs, one, 0, unroll=4)
        pair[j, 1] = dot(p_all[...], g_rows[...])
        pair[j, 0] = dot(ds_all[...], q_rows[...])

    def earlier(j, _):
        backward(j, False)

        @pl.when(top_plane)
        def _():
            part_out[j] = pair[j].astype(jnp.bfloat16)
            part_copy(j, plane - 1).start()

        return 0

    lax.fori_loop(0, plane, earlier, 0)

    def gather_cols(pieces, dst, factor):
        for h in range(group):
            for s in range(splits):
                piece = pieces[h * splits + s]
                if factor is not None:
                    piece = (piece * factor).astype(jnp.bfloat16)
                dst[s * block:(s + 1) * block, h * HEAD_WIDTH:(h + 1) * HEAD_WIDTH] = piece.T

    gather_cols(o_cols, o_buf, None)
    send_out((0,))
    backward(plane, True)
    gather_cols(dq_acc, dq_buf, SCALE)
    send_out((1,))

    @pl.when(plane < planes - 1)
    def _():
        def chain(j, _):
            part_copy(j, plane).wait_recv()
            part_out[j] = (pair[j] + part_in[j].astype(jnp.float32)).astype(jnp.bfloat16)
            part_copy(j, plane - 1).start()
            return 0

        lax.fori_loop(0, plane, chain, 0)
        part_copy(plane, plane).wait_recv()
        pair[plane] += part_in[plane].astype(jnp.float32)

    fin[0] = (pair[plane, 0] * SCALE).astype(jnp.bfloat16)
    fin[1] = pair[plane, 1].astype(jnp.bfloat16)
    send_out((2, 3))

    def drain(d, _):
        p = (me + d) % peers
        for a in (0, 1, 3):
            in_copy(a, me, p).wait_send()

        @pl.when(below)
        def _():
            in_copy(2, me, p).wait_send()

        for a in range(4):
            out_copy(a, me, p).wait_send()
            out_copy(a, p, me).wait_recv()
        return 0

    lax.fori_loop(1, peers, drain, 0)
    for a in range(4):
        own_out(a).wait()

    if staged:
        @pl.when(below & (lane % 2 == 1))
        def _():
            def one(j, _):
                kv_copy(j, plane + 1).wait_send()
                return 0

            lax.fori_loop(0, plane + 1, one, 0)

    def sent(j, _):
        part_copy(j, plane - 1).wait_send()
        return 0

    lax.fori_loop(0, plane, sent, 0)


def hand_over(*refs):
    sources, results, held, sem = refs[:4], refs[4:8], refs[8:12], refs[12]
    loads = [pltpu.make_async_copy(sources[i], held[i], sem.at[0, i]) for i in range(4)]
    stores = [pltpu.make_async_copy(held[i], results[i], sem.at[1, i]) for i in range(4)]
    for load in loads:
        load.start()
    for load, store in zip(loads, stores):
        load.wait()
        store.start()
    for store in stores:
        store.wait()


def shards(query, keys, values, output_gradient):
    ctx = lax.axis_size("ctx")
    tp = lax.axis_size("tp")
    tok, model = query.shape
    kv_heads = keys.shape[1] // HEAD_WIDTH
    group = model // keys.shape[1]
    inner = kv_heads // tp
    planes = ctx // inner
    peers = kv_heads
    chunk = peers * tok
    block = min(256, chunk)
    jobs = group * (chunk // block)
    wide = group * HEAD_WIDTH
    bf16, f32 = jnp.bfloat16, jnp.float32
    anywhere = pl.BlockSpec(memory_space=pl.ANY)
    dma = pltpu.SemaphoreType.DMA
    results = pl.pallas_call(
        functools.partial(kernel, (tp, inner, planes, tok, group, block)),
        out_shape=tuple(
            jax.ShapeDtypeStruct(a.shape, a.dtype) for a in (query, query, keys, values)
        ),
        in_specs=[anywhere] * 4,
        out_specs=(anywhere,) * 4,
        scratch_shapes=[
            pltpu.VMEM((chunk, wide), bf16),
            pltpu.VMEM((chunk, wide), bf16),
            pltpu.VMEM((planes, 2, chunk, HEAD_WIDTH), bf16),
            pltpu.VMEM((chunk, wide), bf16),
            pltpu.VMEM((chunk, wide), bf16),
            pltpu.VMEM((2, chunk, HEAD_WIDTH), bf16),
            pltpu.VMEM((jobs * block, HEAD_WIDTH), bf16),
            pltpu.VMEM((jobs, HEAD_WIDTH, block), bf16),
            pltpu.VMEM((jobs * block, HEAD_WIDTH), bf16),
            pltpu.VMEM((jobs, HEAD_WIDTH, block), bf16),
            pltpu.VMEM((HEAD_WIDTH, chunk), bf16),
            pltpu.VMEM((HEAD_WIDTH, chunk), bf16),
            pltpu.VMEM((jobs, 1, block), f32),
            pltpu.VMEM((jobs, 1, block), f32),
            pltpu.VMEM((jobs, 1, block), f32),
            pltpu.VMEM((jobs, 1, block), f32),
            pltpu.VMEM((jobs, HEAD_WIDTH, block), f32),
            pltpu.VMEM((jobs, HEAD_WIDTH, block), bf16),
            pltpu.VMEM((jobs, HEAD_WIDTH, block), f32),
            pltpu.VMEM((chunk, jobs * block), bf16),
            pltpu.VMEM((chunk, jobs * block), bf16),
            pltpu.VMEM((max(planes - 1, 1), jobs, chunk, block), f32),
            pltpu.VMEM((max(planes - 1, 1), jobs, chunk, block), f32),
            pltpu.VMEM((planes, 2, chunk, HEAD_WIDTH), f32),
            pltpu.VMEM((planes, 2, chunk, HEAD_WIDTH), bf16),
            pltpu.VMEM((planes, 2, chunk, HEAD_WIDTH), bf16),
            dma((8,)),
            dma((4, peers)),
            dma((4, peers)),
            dma((planes,)),
            dma((planes,)),
            dma((planes,)),
            dma((planes,)),
            dma((4, peers)),
            dma((4, peers)),
            pltpu.SemaphoreType.REGULAR,
        ],
        compiler_params=pltpu.CompilerParams(
            collective_id=0, has_side_effects=True, vmem_limit_bytes=64 * 1024 * 1024
        ),
    )(query, keys, values, output_gradient)
    return pl.pallas_call(
        hand_over,
        out_shape=tuple(jax.ShapeDtypeStruct(a.shape, a.dtype) for a in results),
        in_specs=[anywhere] * 4,
        out_specs=(anywhere,) * 4,
        scratch_shapes=[pltpu.VMEM(a.shape, a.dtype) for a in results] + [dma((2, 4))],
        compiler_params=pltpu.CompilerParams(vmem_limit_bytes=64 * 1024 * 1024),
    )(*results)


def solution(mesh):
    placed = (P(("ctx", "tp"), None),) * 4
    return jax.shard_map(
        shards, mesh=mesh, in_specs=placed, out_specs=placed, check_vma=False
    )
```

```python
import functools
import math

import jax
import jax.numpy as jnp
from jax import lax
from jax.experimental import pallas as pl
from jax.experimental.pallas import tpu as pltpu
from jax.sharding import PartitionSpec as P

HEAD_WIDTH = 128
MESH = pl.DeviceIdType.MESH
SCALE = HEAD_WIDTH ** (-0.5)
LOG2_SCALE = SCALE * math.log2(math.e)
MASKED = -1e30


def dot(a, b):
    return jnp.dot(a, b, preferred_element_type=jnp.float32)


def kernel(
    sizes,
    query, keys, values, grads,
    out_ref, dq_ref, dk_ref, dv_ref,
    q_all, g_all, kv_all, o_buf, dq_buf, fin,
    q_rows, q_cols, g_rows, g_cols, k_cols, v_cols,
    row_max, row_sum, lse, delta, acc, o_cols, dq_acc, p_all, ds_all, s_all, dp_all, pair, part_out, part_in,
    own_sem, in_send, in_recv, kv_send, kv_recv, part_send, part_recv, out_send, out_recv, turn_sem,
):
    tp, inner, planes, tok, group, block = sizes
    peers = tp * inner
    chunk = peers * tok
    splits = chunk // block
    jobs = group * splits
    wide = group * HEAD_WIDTH
    ctx_index = lax.axis_index("ctx")
    tp_index = lax.axis_index("tp")
    plane = ctx_index // inner
    lane = ctx_index % inner
    me = lane * tp + tp_index

    def peer_id(p):
        return (plane * inner + p // tp, p % tp)

    def plane_id(z):
        return (z * inner + lane, tp_index)

    barrier = pltpu.get_barrier_semaphore()

    def greet(d, _):
        pl.semaphore_signal(
            barrier, inc=1, device_id=peer_id((me + d) % peers), device_id_type=MESH
        )
        return 0

    lax.fori_loop(1, peers, greet, 0)

    @pl.when(plane > 0)
    def _():
        pl.semaphore_signal(barrier, inc=1, device_id=plane_id(plane - 1), device_id_type=MESH)

    @pl.when(plane < planes - 1)
    def _():
        pl.semaphore_signal(barrier, inc=1, device_id=plane_id(plane + 1), device_id_type=MESH)

    expected = (
        (peers - 1)
        + jnp.where(plane > 0, 1, 0).astype(jnp.int32)
        + jnp.where(plane < planes - 1, 1, 0).astype(jnp.int32)
    )
    pl.semaphore_wait(barrier, expected)

    def cols(p, width):
        return pl.ds(pl.multiple_of(p * width, HEAD_WIDTH), width)

    def rows(p):
        return pl.ds(pl.multiple_of(p * tok, tok), tok)

    def in_pair(a, src_slot, dst_slot):
        if a == 0:
            return keys.at[:, cols(dst_slot, HEAD_WIDTH)], kv_all.at[plane, 0, rows(src_slot), :]
        if a == 1:
            return values.at[:, cols(dst_slot, HEAD_WIDTH)], kv_all.at[plane, 1, rows(src_slot), :]
        if a == 2:
            return query.at[:, cols(dst_slot, wide)], q_all.at[rows(src_slot), :]
        return grads.at[:, cols(dst_slot, wide)], g_all.at[rows(src_slot), :]

    def in_copy(a, src_slot, dst_slot):
        src, dst = in_pair(a, src_slot, dst_slot)
        return pltpu.make_async_remote_copy(
            src_ref=src, dst_ref=dst,
            send_sem=in_send.at[a, dst_slot], recv_sem=in_recv.at[a, src_slot],
            device_id=peer_id(dst_slot), device_id_type=MESH,
        )

    def own_copy(a):
        src, dst = in_pair(a, me, me)
        return pltpu.make_async_copy(src, dst, own_sem.at[a])

    def send_in(arrays):
        def one(d, _):
            for a in arrays:
                in_copy(a, me, (me + d) % peers).start()
            return 0

        lax.fori_loop(1, peers, one, 0)

    def await_in(arrays):
        for a in arrays:
            own_copy(a).wait()

        def one(d, _):
            for a in arrays:
                in_copy(a, (me + d) % peers, me).wait_recv()
            return 0

        lax.fori_loop(1, peers, one, 0)

    for a in range(4):
        own_copy(a).start()
    send_in((0, 1))

    def kv_copy(j, half, target):
        return pltpu.make_async_remote_copy(
            src_ref=kv_all.at[j, half], dst_ref=kv_all.at[j, half],
            send_sem=kv_send.at[j, half], recv_sem=kv_recv.at[j, half],
            device_id=plane_id(target), device_id_type=MESH,
        )

    await_in((0, 1))
    top_plane = plane == planes - 1

    staged = inner % 2 == 0
    leads = lane % 2 == 0 if staged else lane == lane
    below = plane < planes - 1

    def relay():
        def one(n, _):
            j = plane - 1 - n
            for half in range(2):
                kv_copy(j, half, plane).wait_recv()
                kv_copy(j, half, plane + 1).start()
            return 0

        lax.fori_loop(0, plane, one, 0)

    @pl.when(below & leads)
    def _():
        for half in range(2):
            kv_copy(plane, half, plane + 1).start()

    send_in((2,))

    @pl.when(top_plane)
    def _():
        def left(d, _):
            in_copy(2, me, (me + d) % peers).wait_send()
            return 0

        lax.fori_loop(1, peers, left, 0)

    send_in((3,))

    @pl.when(below & leads)
    def _():
        relay()

        def gone(j, _):
            for half in range(2):
                kv_copy(j, half, plane + 1).wait_send()
            return 0

        lax.fori_loop(0, plane + 1, gone, 0)
        if staged:
            pl.semaphore_signal(
                turn_sem, inc=1, device_id=(ctx_index + 1, tp_index), device_id_type=MESH
            )

    if staged:
        @pl.when(below & (lane % 2 == 1))
        def _():
            pl.semaphore_wait(turn_sem, 1)
            for half in range(2):
                kv_copy(plane, half, plane + 1).start()
            relay()

    def spread(whole, by_rows, by_cols):
        for h in range(group):
            for s in range(splits):
                piece = whole[s * block:(s + 1) * block, h * HEAD_WIDTH:(h + 1) * HEAD_WIDTH]
                by_rows[(h * splits + s) * block:(h * splits + s + 1) * block] = piece
                by_cols[h * splits + s] = piece.T

    await_in((2,))
    spread(q_all, q_rows, q_cols)

    def masked(s, split):
        shape = s.shape
        key_pos = lax.broadcasted_iota(jnp.int32, shape, 0)
        query_pos = lax.broadcasted_iota(jnp.int32, shape, 1) + split * block
        return jnp.where(key_pos <= query_pos, s, MASKED)

    v_cols[...] = kv_all[plane, 1].T

    def first(h, _):
        for split in range(splits):
            i, seen = h * splits + split, (split + 1) * block
            s = masked(dot(kv_all[plane, 0, :seen], q_cols[i]) * LOG2_SCALE, split)
            s_all[plane, i, :seen] = s
            top = jnp.max(s, axis=0, keepdims=True)
            p = jnp.exp2(s - top)
            row_max[i] = top
            row_sum[i] = jnp.sum(p, axis=0, keepdims=True)
            acc[i] = dot(v_cols[:, :seen], p.astype(jnp.bfloat16))
        return 0

    lax.fori_loop(0, group, first, 0, unroll=2)

    await_in((3,))
    spread(g_all, g_rows, g_cols)

    def first_dp(h, _):
        for split in range(splits):
            i, seen = h * splits + split, (split + 1) * block
            dp_all[plane, i, :seen] = dot(kv_all[plane, 1, :seen], g_cols[i])
        return 0

    lax.fori_loop(0, group, first_dp, 0, unroll=2)

    def forward(n, _):
        j = plane - 1 - n

        @pl.when(top_plane)
        def _():
            for half in range(2):
                kv_copy(j, half, plane).wait_recv()

        v_cols[...] = kv_all[j, 1].T

        def one(i, _):
            s = dot(kv_all[j, 0], q_cols[i]) * LOG2_SCALE
            s_all[j, i] = s
            dp_all[j, i] = dot(kv_all[j, 1], g_cols[i])
            old = row_max[i]
            top = jnp.maximum(old, jnp.max(s, axis=0, keepdims=True))
            p = jnp.exp2(s - top)
            shrink = jnp.exp2(old - top)
            row_max[i] = top
            row_sum[i] = row_sum[i] * shrink + jnp.sum(p, axis=0, keepdims=True)
            acc[i] = acc[i] * shrink + dot(v_cols[...], p.astype(jnp.bfloat16))
            return 0

        lax.fori_loop(0, jobs, one, 0, unroll=4)
        return 0

    lax.fori_loop(0, plane, forward, 0)

    for i in range(jobs):
        total = row_sum[i]
        rounded = (acc[i] / total).astype(jnp.bfloat16)
        o_cols[i] = rounded
        lse[i] = row_max[i] + jnp.log2(total)
        delta[i] = jnp.sum(
            g_cols[i].astype(jnp.float32) * rounded.astype(jnp.float32), axis=0, keepdims=True
        )

    def out_pair(a, src_slot, dst_slot):
        if a == 0:
            return o_buf.at[rows(dst_slot), :], out_ref.at[:, cols(src_slot, wide)]
        if a == 1:
            return dq_buf.at[rows(dst_slot), :], dq_ref.at[:, cols(src_slot, wide)]
        if a == 2:
            return fin.at[0, rows(dst_slot), :], dk_ref.at[:, cols(src_slot, HEAD_WIDTH)]
        return fin.at[1, rows(dst_slot), :], dv_ref.at[:, cols(src_slot, HEAD_WIDTH)]

    def out_copy(a, src_slot, dst_slot):
        src, dst = out_pair(a, src_slot, dst_slot)
        return pltpu.make_async_remote_copy(
            src_ref=src, dst_ref=dst,
            send_sem=out_send.at[a, dst_slot], recv_sem=out_recv.at[a, src_slot],
            device_id=peer_id(dst_slot), device_id_type=MESH,
        )

    def own_out(a):
        src, dst = out_pair(a, me, me)
        return pltpu.make_async_copy(src, dst, own_sem.at[4 + a])

    def send_out(arrays):
        for a in arrays:
            own_out(a).start()

        def one(d, _):
            for a in arrays:
                out_copy(a, me, (me + d) % peers).start()
            return 0

        lax.fori_loop(1, peers, one, 0)

    dq_acc[...] = jnp.zeros_like(dq_acc)

    def part_copy(j, half, target):
        return pltpu.make_async_remote_copy(
            src_ref=part_out.at[j, half], dst_ref=part_in.at[j, half],
            send_sem=part_send.at[j, half], recv_sem=part_recv.at[j, half],
            device_id=plane_id(target), device_id_type=MESH,
        )

    def gradients(j, i, seen):
        where = pl.ds(i * block if isinstance(i, int) else pl.multiple_of(i * block, block), block)
        p = jnp.exp2(s_all[j, i, :seen] - lse[i])
        ds = (p * (dp_all[j, i, :seen] - delta[i])).astype(jnp.bfloat16)
        p_all[:seen, where] = p.astype(jnp.bfloat16)
        ds_all[:seen, where] = ds
        if seen < chunk:
            unseen = jnp.zeros((chunk - seen, block), jnp.bfloat16)
            p_all[seen:, where] = unseen
            ds_all[seen:, where] = unseen
        dq_acc[i] += dot(k_cols[:, :seen], ds)

    def backward(j, diagonal):
        k_cols[...] = kv_all[j, 0].T

        def one(i, _):
            gradients(j, i, chunk)
            return 0

        def triangle(h, _):
            for split in range(splits):
                gradients(j, h * splits + split, (split + 1) * block)
            return 0

        if diagonal:
            lax.fori_loop(0, group, triangle, 0, unroll=2)
        else:
            lax.fori_loop(0, jobs, one, 0, unroll=4)
        for half, weights, lines in ((1, p_all, g_rows), (0, ds_all, q_rows)):
            pair[j, half] = dot(weights[...], lines[...])
            if not diagonal:
                @pl.when(top_plane)
                def _():
                    part_out[j, half] = pair[j, half].astype(jnp.bfloat16)
                    part_copy(j, half, plane - 1).start()

    def earlier(j, _):
        backward(j, False)
        return 0

    lax.fori_loop(0, plane, earlier, 0)

    def gather_cols(pieces, dst, factor):
        for h in range(group):
            for s in range(splits):
                piece = pieces[h * splits + s]
                if factor is not None:
                    piece = (piece * factor).astype(jnp.bfloat16)
                dst[s * block:(s + 1) * block, h * HEAD_WIDTH:(h + 1) * HEAD_WIDTH] = piece.T

    gather_cols(o_cols, o_buf, None)
    send_out((0,))
    backward(plane, True)
    gather_cols(dq_acc, dq_buf, SCALE)
    send_out((1,))

    @pl.when(below)
    def _():
        def chain(j, _):
            for half in (1, 0):
                part_copy(j, half, plane).wait_recv()
                whole = pair[j, half] + part_in[j, half].astype(jnp.float32)
                part_out[j, half] = whole.astype(jnp.bfloat16)
                part_copy(j, half, plane - 1).start()
            return 0

        lax.fori_loop(0, plane, chain, 0)

    for half, factor in ((1, 1.0), (0, SCALE)):
        @pl.when(below)
        def _():
            part_copy(plane, half, plane).wait_recv()
            pair[plane, half] += part_in[plane, half].astype(jnp.float32)

        fin[half] = (pair[plane, half] * factor).astype(jnp.bfloat16)
        send_out((2 + half,))

    def drain(d, _):
        p = (me + d) % peers
        for a in (0, 1, 3):
            in_copy(a, me, p).wait_send()

        @pl.when(below)
        def _():
            in_copy(2, me, p).wait_send()

        for a in range(4):
            out_copy(a, me, p).wait_send()
            out_copy(a, p, me).wait_recv()
        return 0

    lax.fori_loop(1, peers, drain, 0)
    for a in range(4):
        own_out(a).wait()

    if staged:
        @pl.when(below & (lane % 2 == 1))
        def _():
            def one(j, _):
                for half in range(2):
                    kv_copy(j, half, plane + 1).wait_send()
                return 0

            lax.fori_loop(0, plane + 1, one, 0)

    def sent(j, _):
        for half in range(2):
            part_copy(j, half, plane - 1).wait_send()
        return 0

    lax.fori_loop(0, plane, sent, 0)


def hand_over(*refs):
    sources, results, held, sem = refs[:4], refs[4:8], refs[8:12], refs[12]
    loads = [pltpu.make_async_copy(sources[i], held[i], sem.at[0, i]) for i in range(4)]
    stores = [pltpu.make_async_copy(held[i], results[i], sem.at[1, i]) for i in range(4)]
    for load in loads:
        load.start()
    for load, store in zip(loads, stores):
        load.wait()
        store.start()
    for store in stores:
        store.wait()


def shards(query, keys, values, output_gradient):
    ctx = lax.axis_size("ctx")
    tp = lax.axis_size("tp")
    tok, model = query.shape
    kv_heads = keys.shape[1] // HEAD_WIDTH
    group = model // keys.shape[1]
    inner = kv_heads // tp
    planes = ctx // inner
    peers = kv_heads
    chunk = peers * tok
    block = min(256, chunk)
    jobs = group * (chunk // block)
    wide = group * HEAD_WIDTH
    bf16, f32 = jnp.bfloat16, jnp.float32
    anywhere = pl.BlockSpec(memory_space=pl.ANY)
    dma = pltpu.SemaphoreType.DMA
    results = pl.pallas_call(
        functools.partial(kernel, (tp, inner, planes, tok, group, block)),
        out_shape=tuple(
            jax.ShapeDtypeStruct(a.shape, a.dtype) for a in (query, query, keys, values)
        ),
        in_specs=[anywhere] * 4,
        out_specs=(anywhere,) * 4,
        scratch_shapes=[
            pltpu.VMEM((chunk, wide), bf16),
            pltpu.VMEM((chunk, wide), bf16),
            pltpu.VMEM((planes, 2, chunk, HEAD_WIDTH), bf16),
            pltpu.VMEM((chunk, wide), bf16),
            pltpu.VMEM((chunk, wide), bf16),
            pltpu.VMEM((2, chunk, HEAD_WIDTH), bf16),
            pltpu.VMEM((jobs * block, HEAD_WIDTH), bf16),
            pltpu.VMEM((jobs, HEAD_WIDTH, block), bf16),
            pltpu.VMEM((jobs * block, HEAD_WIDTH), bf16),
            pltpu.VMEM((jobs, HEAD_WIDTH, block), bf16),
            pltpu.VMEM((HEAD_WIDTH, chunk), bf16),
            pltpu.VMEM((HEAD_WIDTH, chunk), bf16),
            pltpu.VMEM((jobs, 1, block), f32),
            pltpu.VMEM((jobs, 1, block), f32),
            pltpu.VMEM((jobs, 1, block), f32),
            pltpu.VMEM((jobs, 1, block), f32),
            pltpu.VMEM((jobs, HEAD_WIDTH, block), f32),
            pltpu.VMEM((jobs, HEAD_WIDTH, block), bf16),
            pltpu.VMEM((jobs, HEAD_WIDTH, block), f32),
            pltpu.VMEM((chunk, jobs * block), bf16),
            pltpu.VMEM((chunk, jobs * block), bf16),
            pltpu.VMEM((planes, jobs, chunk, block), f32),
            pltpu.VMEM((planes, jobs, chunk, block), f32),
            pltpu.VMEM((planes, 2, chunk, HEAD_WIDTH), f32),
            pltpu.VMEM((planes, 2, chunk, HEAD_WIDTH), bf16),
            pltpu.VMEM((planes, 2, chunk, HEAD_WIDTH), bf16),
            dma((8,)),
            dma((4, peers)),
            dma((4, peers)),
            dma((planes, 2)),
            dma((planes, 2)),
            dma((planes, 2)),
            dma((planes, 2)),
            dma((4, peers)),
            dma((4, peers)),
            pltpu.SemaphoreType.REGULAR,
        ],
        compiler_params=pltpu.CompilerParams(
            collective_id=0, has_side_effects=True, vmem_limit_bytes=64 * 1024 * 1024
        ),
    )(query, keys, values, output_gradient)
    return pl.pallas_call(
        hand_over,
        out_shape=tuple(jax.ShapeDtypeStruct(a.shape, a.dtype) for a in results),
        in_specs=[anywhere] * 4,
        out_specs=(anywhere,) * 4,
        scratch_shapes=[pltpu.VMEM(a.shape, a.dtype) for a in results] + [dma((2, 4))],
        compiler_params=pltpu.CompilerParams(vmem_limit_bytes=64 * 1024 * 1024),
    )(*results)


def solution(mesh):
    placed = (P(("ctx", "tp"), None),) * 4
    return jax.shard_map(
        shards, mesh=mesh, in_specs=placed, out_specs=placed, check_vma=False
    )
```

```python
import functools
import math

import jax
import jax.numpy as jnp
from jax import lax
from jax.experimental import pallas as pl
from jax.experimental.pallas import tpu as pltpu
from jax.sharding import PartitionSpec as P

HEAD_WIDTH = 128
MESH = pl.DeviceIdType.MESH
SCALE = HEAD_WIDTH ** (-0.5)
LOG2_SCALE = SCALE * math.log2(math.e)
MASKED = -1e30


def dot(a, b):
    return jnp.dot(a, b, preferred_element_type=jnp.float32)


def kernel(
    sizes,
    query, keys, values, grads,
    out_ref, dq_ref, dk_ref, dv_ref,
    q_all, g_all, kv_all, o_buf, dq_buf, fin,
    q_rows, q_cols, g_rows, g_cols, k_cols, v_cols,
    row_max, row_sum, lse, delta, acc, o_cols, dq_acc, p_all, ds_all, s_all, dp_all, pair, part_out, part_in,
    own_sem, in_send, in_recv, kv_send, kv_recv, part_send, part_recv, out_send, out_recv, turn_sem,
):
    tp, inner, planes, tok, group, block = sizes
    peers = tp * inner
    chunk = peers * tok
    splits = chunk // block
    jobs = group * splits
    wide = group * HEAD_WIDTH
    ctx_index = lax.axis_index("ctx")
    tp_index = lax.axis_index("tp")
    plane = ctx_index // inner
    lane = ctx_index % inner
    me = lane * tp + tp_index

    def peer_id(p):
        return (plane * inner + p // tp, p % tp)

    def plane_id(z):
        return (z * inner + lane, tp_index)

    barrier = pltpu.get_barrier_semaphore()

    def greet(d, _):
        pl.semaphore_signal(
            barrier, inc=1, device_id=peer_id((me + d) % peers), device_id_type=MESH
        )
        return 0

    lax.fori_loop(1, peers, greet, 0)

    @pl.when(plane > 0)
    def _():
        pl.semaphore_signal(barrier, inc=1, device_id=plane_id(plane - 1), device_id_type=MESH)

    @pl.when(plane < planes - 1)
    def _():
        pl.semaphore_signal(barrier, inc=1, device_id=plane_id(plane + 1), device_id_type=MESH)

    expected = (
        (peers - 1)
        + jnp.where(plane > 0, 1, 0).astype(jnp.int32)
        + jnp.where(plane < planes - 1, 1, 0).astype(jnp.int32)
    )
    pl.semaphore_wait(barrier, expected)

    def cols(p, width):
        return pl.ds(pl.multiple_of(p * width, HEAD_WIDTH), width)

    def rows(p):
        return pl.ds(pl.multiple_of(p * tok, tok), tok)

    def in_pair(a, src_slot, dst_slot):
        if a == 0:
            return keys.at[:, cols(dst_slot, HEAD_WIDTH)], kv_all.at[plane, 0, rows(src_slot), :]
        if a == 1:
            return values.at[:, cols(dst_slot, HEAD_WIDTH)], kv_all.at[plane, 1, rows(src_slot), :]
        if a == 2:
            return query.at[:, cols(dst_slot, wide)], q_all.at[rows(src_slot), :]
        return grads.at[:, cols(dst_slot, wide)], g_all.at[rows(src_slot), :]

    def in_copy(a, src_slot, dst_slot):
        src, dst = in_pair(a, src_slot, dst_slot)
        return pltpu.make_async_remote_copy(
            src_ref=src, dst_ref=dst,
            send_sem=in_send.at[a, dst_slot], recv_sem=in_recv.at[a, src_slot],
            device_id=peer_id(dst_slot), device_id_type=MESH,
        )

    def own_copy(a):
        src, dst = in_pair(a, me, me)
        return pltpu.make_async_copy(src, dst, own_sem.at[a])

    def send_in(arrays):
        def one(d, _):
            for a in arrays:
                in_copy(a, me, (me + d) % peers).start()
            return 0

        lax.fori_loop(1, peers, one, 0)

    def await_in(arrays):
        for a in arrays:
            own_copy(a).wait()

        def one(d, _):
            for a in arrays:
                in_copy(a, (me + d) % peers, me).wait_recv()
            return 0

        lax.fori_loop(1, peers, one, 0)

    for a in range(4):
        own_copy(a).start()
    send_in((0, 1))

    def kv_copy(j, half, target):
        return pltpu.make_async_remote_copy(
            src_ref=kv_all.at[j, half], dst_ref=kv_all.at[j, half],
            send_sem=kv_send.at[j, half], recv_sem=kv_recv.at[j, half],
            device_id=plane_id(target), device_id_type=MESH,
        )

    await_in((0, 1))
    top_plane = plane == planes - 1

    staged = inner % 2 == 0
    leads = lane % 2 == 0 if staged else lane == lane
    below = plane < planes - 1

    def relay():
        def one(n, _):
            j = plane - 1 - n
            for half in range(2):
                kv_copy(j, half, plane).wait_recv()
                kv_copy(j, half, plane + 1).start()
            return 0

        lax.fori_loop(0, plane, one, 0)

    @pl.when(below & leads)
    def _():
        for half in range(2):
            kv_copy(plane, half, plane + 1).start()

    send_in((2,))

    @pl.when(top_plane)
    def _():
        def left(d, _):
            in_copy(2, me, (me + d) % peers).wait_send()
            return 0

        lax.fori_loop(1, peers, left, 0)

    send_in((3,))

    @pl.when(below & leads)
    def _():
        relay()

        def gone(j, _):
            for half in range(2):
                kv_copy(j, half, plane + 1).wait_send()
            return 0

        lax.fori_loop(0, plane + 1, gone, 0)
        if staged:
            pl.semaphore_signal(
                turn_sem, inc=1, device_id=(ctx_index + 1, tp_index), device_id_type=MESH
            )

    if staged:
        @pl.when(below & (lane % 2 == 1))
        def _():
            pl.semaphore_wait(turn_sem, 1)
            for half in range(2):
                kv_copy(plane, half, plane + 1).start()
            relay()

    def spread(whole, by_rows, by_cols):
        for h in range(group):
            for s in range(splits):
                piece = whole[s * block:(s + 1) * block, h * HEAD_WIDTH:(h + 1) * HEAD_WIDTH]
                by_rows[(h * splits + s) * block:(h * splits + s + 1) * block] = piece
                by_cols[h * splits + s] = piece.T

    await_in((2,))
    spread(q_all, q_rows, q_cols)

    def masked(s, split):
        shape = s.shape
        key_pos = lax.broadcasted_iota(jnp.int32, shape, 0)
        query_pos = lax.broadcasted_iota(jnp.int32, shape, 1) + split * block
        return jnp.where(key_pos <= query_pos, s, MASKED)

    v_cols[...] = kv_all[plane, 1].T

    def first(h, _):
        for split in range(splits):
            i, seen = h * splits + split, (split + 1) * block
            s = masked(dot(kv_all[plane, 0, :seen], q_cols[i]) * LOG2_SCALE, split)
            top = jnp.max(s, axis=0, keepdims=True)
            p = jnp.exp2(s - top)
            row_max[i] = top
            row_sum[i] = jnp.sum(p, axis=0, keepdims=True)
            acc[i] = dot(v_cols[:, :seen], p.astype(jnp.bfloat16))
        return 0

    lax.fori_loop(0, group, first, 0, unroll=2)

    await_in((3,))
    spread(g_all, g_rows, g_cols)

    def forward(n, _):
        j = plane - 1 - n

        @pl.when(top_plane)
        def _():
            for half in range(2):
                kv_copy(j, half, plane).wait_recv()

        v_cols[...] = kv_all[j, 1].T

        def one(i, _):
            s = dot(kv_all[j, 0], q_cols[i]) * LOG2_SCALE
            s_all[j, i] = s
            dp_all[j, i] = dot(kv_all[j, 1], g_cols[i])
            old = row_max[i]
            top = jnp.maximum(old, jnp.max(s, axis=0, keepdims=True))
            p = jnp.exp2(s - top)
            shrink = jnp.exp2(old - top)
            row_max[i] = top
            row_sum[i] = row_sum[i] * shrink + jnp.sum(p, axis=0, keepdims=True)
            acc[i] = acc[i] * shrink + dot(v_cols[...], p.astype(jnp.bfloat16))
            return 0

        lax.fori_loop(0, jobs, one, 0, unroll=4)
        return 0

    lax.fori_loop(0, plane, forward, 0)

    for i in range(jobs):
        total = row_sum[i]
        rounded = (acc[i] / total).astype(jnp.bfloat16)
        o_cols[i] = rounded
        lse[i] = row_max[i] + jnp.log2(total)
        delta[i] = jnp.sum(
            g_cols[i].astype(jnp.float32) * rounded.astype(jnp.float32), axis=0, keepdims=True
        )

    def out_pair(a, src_slot, dst_slot):
        if a == 0:
            return o_buf.at[rows(dst_slot), :], out_ref.at[:, cols(src_slot, wide)]
        if a == 1:
            return dq_buf.at[rows(dst_slot), :], dq_ref.at[:, cols(src_slot, wide)]
        if a == 2:
            return fin.at[0, rows(dst_slot), :], dk_ref.at[:, cols(src_slot, HEAD_WIDTH)]
        return fin.at[1, rows(dst_slot), :], dv_ref.at[:, cols(src_slot, HEAD_WIDTH)]

    def out_copy(a, src_slot, dst_slot):
        src, dst = out_pair(a, src_slot, dst_slot)
        return pltpu.make_async_remote_copy(
            src_ref=src, dst_ref=dst,
            send_sem=out_send.at[a, dst_slot], recv_sem=out_recv.at[a, src_slot],
            device_id=peer_id(dst_slot), device_id_type=MESH,
        )

    def own_out(a):
        src, dst = out_pair(a, me, me)
        return pltpu.make_async_copy(src, dst, own_sem.at[4 + a])

    def send_out(arrays):
        for a in arrays:
            own_out(a).start()

        def one(d, _):
            for a in arrays:
                out_copy(a, me, (me + d) % peers).start()
            return 0

        lax.fori_loop(1, peers, one, 0)

    dq_acc[...] = jnp.zeros_like(dq_acc)

    def part_copy(j, half, target):
        return pltpu.make_async_remote_copy(
            src_ref=part_out.at[j, half], dst_ref=part_in.at[j, half],
            send_sem=part_send.at[j, half], recv_sem=part_recv.at[j, half],
            device_id=plane_id(target), device_id_type=MESH,
        )

    def gradients(j, i, seen, split):
        where = pl.ds(i * block if isinstance(i, int) else pl.multiple_of(i * block, block), block)
        if split is not None:
            s = masked(dot(kv_all[j, 0, :seen], q_cols[i]) * LOG2_SCALE, split)
            dp = dot(kv_all[j, 1, :seen], g_cols[i])
        else:
            s, dp = s_all[j, i], dp_all[j, i]
        p = jnp.exp2(s - lse[i])
        ds = (p * (dp - delta[i])).astype(jnp.bfloat16)
        p_all[:seen, where] = p.astype(jnp.bfloat16)
        ds_all[:seen, where] = ds
        if seen < chunk:
            unseen = jnp.zeros((chunk - seen, block), jnp.bfloat16)
            p_all[seen:, where] = unseen
            ds_all[seen:, where] = unseen
        dq_acc[i] += dot(k_cols[:, :seen], ds)

    def backward(j, diagonal):
        k_cols[...] = kv_all[j, 0].T

        def one(i, _):
            gradients(j, i, chunk, None)
            return 0

        def triangle(h, _):
            for split in range(splits):
                gradients(j, h * splits + split, (split + 1) * block, split)
            return 0

        if diagonal:
            lax.fori_loop(0, group, triangle, 0, unroll=2)
        else:
            lax.fori_loop(0, jobs, one, 0, unroll=4)
        pair[j, 1] = dot(p_all[...], g_rows[...])
        pair[j, 0] = dot(ds_all[...], q_rows[...])

    def earlier(j, _):
        backward(j, False)

        @pl.when(top_plane)
        def _():
            for half in (1, 0):
                part_out[j, half] = pair[j, half].astype(jnp.bfloat16)
                part_copy(j, half, plane - 1).start()

        return 0

    lax.fori_loop(0, plane, earlier, 0)

    def gather_cols(pieces, dst, factor):
        for h in range(group):
            for s in range(splits):
                piece = pieces[h * splits + s]
                if factor is not None:
                    piece = (piece * factor).astype(jnp.bfloat16)
                dst[s * block:(s + 1) * block, h * HEAD_WIDTH:(h + 1) * HEAD_WIDTH] = piece.T

    gather_cols(o_cols, o_buf, None)
    send_out((0,))
    backward(plane, True)
    gather_cols(dq_acc, dq_buf, SCALE)
    send_out((1,))

    @pl.when(below)
    def _():
        def chain(j, _):
            for half in (1, 0):
                part_copy(j, half, plane).wait_recv()
                whole = pair[j, half] + part_in[j, half].astype(jnp.float32)
                part_out[j, half] = whole.astype(jnp.bfloat16)
                part_copy(j, half, plane - 1).start()
            return 0

        lax.fori_loop(0, plane, chain, 0)

    for half, factor in ((1, 1.0), (0, SCALE)):
        @pl.when(below)
        def _():
            part_copy(plane, half, plane).wait_recv()
            pair[plane, half] += part_in[plane, half].astype(jnp.float32)

        fin[half] = (pair[plane, half] * factor).astype(jnp.bfloat16)
        send_out((2 + half,))

    def drain(d, _):
        p = (me + d) % peers
        for a in (0, 1, 3):
            in_copy(a, me, p).wait_send()

        @pl.when(below)
        def _():
            in_copy(2, me, p).wait_send()

        for a in range(4):
            out_copy(a, me, p).wait_send()
            out_copy(a, p, me).wait_recv()
        return 0

    lax.fori_loop(1, peers, drain, 0)
    for a in range(4):
        own_out(a).wait()

    if staged:
        @pl.when(below & (lane % 2 == 1))
        def _():
            def one(j, _):
                for half in range(2):
                    kv_copy(j, half, plane + 1).wait_send()
                return 0

            lax.fori_loop(0, plane + 1, one, 0)

    def sent(j, _):
        for half in range(2):
            part_copy(j, half, plane - 1).wait_send()
        return 0

    lax.fori_loop(0, plane, sent, 0)


def hand_over(*refs):
    sources, results, held, sem = refs[:4], refs[4:8], refs[8:12], refs[12]
    loads = [pltpu.make_async_copy(sources[i], held[i], sem.at[0, i]) for i in range(4)]
    stores = [pltpu.make_async_copy(held[i], results[i], sem.at[1, i]) for i in range(4)]
    for load in loads:
        load.start()
    for load, store in zip(loads, stores):
        load.wait()
        store.start()
    for store in stores:
        store.wait()


def shards(query, keys, values, output_gradient):
    ctx = lax.axis_size("ctx")
    tp = lax.axis_size("tp")
    tok, model = query.shape
    kv_heads = keys.shape[1] // HEAD_WIDTH
    group = model // keys.shape[1]
    inner = kv_heads // tp
    planes = ctx // inner
    peers = kv_heads
    chunk = peers * tok
    block = min(256, chunk)
    jobs = group * (chunk // block)
    wide = group * HEAD_WIDTH
    bf16, f32 = jnp.bfloat16, jnp.float32
    anywhere = pl.BlockSpec(memory_space=pl.ANY)
    dma = pltpu.SemaphoreType.DMA
    results = pl.pallas_call(
        functools.partial(kernel, (tp, inner, planes, tok, group, block)),
        out_shape=tuple(
            jax.ShapeDtypeStruct(a.shape, a.dtype) for a in (query, query, keys, values)
        ),
        in_specs=[anywhere] * 4,
        out_specs=(anywhere,) * 4,
        scratch_shapes=[
            pltpu.VMEM((chunk, wide), bf16),
            pltpu.VMEM((chunk, wide), bf16),
            pltpu.VMEM((planes, 2, chunk, HEAD_WIDTH), bf16),
            pltpu.VMEM((chunk, wide), bf16),
            pltpu.VMEM((chunk, wide), bf16),
            pltpu.VMEM((2, chunk, HEAD_WIDTH), bf16),
            pltpu.VMEM((jobs * block, HEAD_WIDTH), bf16),
            pltpu.VMEM((jobs, HEAD_WIDTH, block), bf16),
            pltpu.VMEM((jobs * block, HEAD_WIDTH), bf16),
            pltpu.VMEM((jobs, HEAD_WIDTH, block), bf16),
            pltpu.VMEM((HEAD_WIDTH, chunk), bf16),
            pltpu.VMEM((HEAD_WIDTH, chunk), bf16),
            pltpu.VMEM((jobs, 1, block), f32),
            pltpu.VMEM((jobs, 1, block), f32),
            pltpu.VMEM((jobs, 1, block), f32),
            pltpu.VMEM((jobs, 1, block), f32),
            pltpu.VMEM((jobs, HEAD_WIDTH, block), f32),
            pltpu.VMEM((jobs, HEAD_WIDTH, block), bf16),
            pltpu.VMEM((jobs, HEAD_WIDTH, block), f32),
            pltpu.VMEM((chunk, jobs * block), bf16),
            pltpu.VMEM((chunk, jobs * block), bf16),
            pltpu.VMEM((max(planes - 1, 1), jobs, chunk, block), f32),
            pltpu.VMEM((max(planes - 1, 1), jobs, chunk, block), f32),
            pltpu.VMEM((planes, 2, chunk, HEAD_WIDTH), f32),
            pltpu.VMEM((planes, 2, chunk, HEAD_WIDTH), bf16),
            pltpu.VMEM((planes, 2, chunk, HEAD_WIDTH), bf16),
            dma((8,)),
            dma((4, peers)),
            dma((4, peers)),
            dma((planes, 2)),
            dma((planes, 2)),
            dma((planes, 2)),
            dma((planes, 2)),
            dma((4, peers)),
            dma((4, peers)),
            pltpu.SemaphoreType.REGULAR,
        ],
        compiler_params=pltpu.CompilerParams(
            collective_id=0, has_side_effects=True, vmem_limit_bytes=64 * 1024 * 1024
        ),
    )(query, keys, values, output_gradient)
    return pl.pallas_call(
        hand_over,
        out_shape=tuple(jax.ShapeDtypeStruct(a.shape, a.dtype) for a in results),
        in_specs=[anywhere] * 4,
        out_specs=(anywhere,) * 4,
        scratch_shapes=[pltpu.VMEM(a.shape, a.dtype) for a in results] + [dma((2, 4))],
        compiler_params=pltpu.CompilerParams(vmem_limit_bytes=64 * 1024 * 1024),
    )(*results)


def solution(mesh):
    placed = (P(("ctx", "tp"), None),) * 4
    return jax.shard_map(
        shards, mesh=mesh, in_specs=placed, out_specs=placed, check_vma=False
    )
```
